512 devices in a mesh: bins: 64 (over z, y), freq: 8 (over x, core).
Axes of the slice: x: 4, y: 4, z: 16, core: 2. Of those that a mesh axis runs over, the one named last changes fastest.
Arguments:
- traces: bfloat16 [2000, 524288], P('freq', 'bins'), may hold values from -6 to 6
- bin_ids: int32 [524288], P('bins'), may hold values from 0 to 1023
- valid: int32 [524288], P('bins'), may hold values 0 or 1
- tile_owner: int32 [4096, 1], P('bins'), may hold values from 0 to 63; in each aligned block of 64 rows (0 to 63, 64 to 127, ...) at most 2 rows name the same one
Outputs:
- rebuilt: float32 [512, 2, 65536], P(('bins', 'freq'))
The draws below stay inside these ranges and needn't reach their ends.
Inputs may be any that keep to these rules, and one draw needn't show every extreme that they name: `tile_owner`: within the tiles of one shot group (aligned blocks of 64 tiles) no owner is named by more than 2 tiles.
All inputs are finite; a program needn't handle non-finite values. No bound on the sum of `valid` on one device may be relied on, other than what follows from the above.
Results may differ from the reference program's by a relative error of at most 0.0038.
Values may be sent and summed in bfloat16 or wider, within the bound.
A program may use at most 128 MiB of HBM per device.

```python
import math
import jax
import jax.numpy as jnp
import numpy as np
from jax import lax

MX = 16
MY = 16
HX = 16
HY = 16
NT = 2000
TILE = 128
TILES_DEV = 64
ITERS = 2
CAP = 2
TILES = 4096
TRACES = 524288
LB = 1024
NF = 512
N_BINS = 64
N_FREQ = 8


def shared_bins(key):
    bin_numbers = jax.random.randint(key, (TRACES,), 0, LB, dtype=jnp.int32)
    return bin_numbers.at[0].set(0).at[1].set(LB - 1)


def silent_table(key):
    group_count = TRACES // (TILES_DEV * TILE)
    marks = jax.random.randint(jax.random.fold_in(key, 11), (group_count, LB), 0, 4, dtype=jnp.int32)
    return marks == 0


def draw_bin_ids(key, part):
    return shared_bins(key)


def draw_traces(key, part):
    bin_numbers = shared_bins(key)
    silent = silent_table(key)
    key = jax.random.fold_in(key, 5)
    trace_group = jnp.arange(TRACES, dtype=jnp.int32) // (TILES_DEV * TILE)
    silent_trace = silent[trace_group, bin_numbers]
    live_mask = jnp.where(silent_trace, 0.0, 1.0).astype(jnp.float32)
    values = jnp.clip(jax.random.normal(key, (NT, TRACES), jnp.float32), -6.0, 6.0)
    return (values * live_mask[None, :]).astype(jnp.bfloat16)


def with_ends(entries, key, least, largest):
    longest = entries.shape.index(max(entries.shape))
    spots = []
    for shift in (0, 1):
        where = [jax.random.randint(jax.random.fold_in(key, axis), (), 0, length) for axis, length in enumerate(entries.shape)]
        where[longest] = (where[longest] + shift) % entries.shape[longest]
        spots.append(tuple(where))
    return entries.at[spots[0]].set(least).at[spots[1]].set(largest)


def assign_block(key, own, number, rows, number_of, top, bound, slope):
    ranking = jax.random.permutation(key, number_of)
    packed, common = portions_of(number_of, rows * top, bound, slope, True), portions_of(number_of, rows * top, bound, slope, False)
    places = jnp.arange(number_of)

    def named(sizes, turn):
        used = int((sizes > 0).sum())
        fixed = max(1, used // 4)
        moved = fixed + (places - fixed + turn * (used - fixed)) % max(1, number_of - fixed)
        return jnp.zeros((number_of,), jnp.int32).at[ranking[jnp.where(places < fixed, places, moved)]].set(jnp.asarray(sizes, jnp.int32))

    sizes = jnp.where(number % 4 == 0, named(packed, number // 4), named(common, number - number // 4 - 1))
    mixed = jax.random.permutation(jax.random.fold_in(own, 3), number_of)
    donor, taker = mixed[0:number_of // 2 * 2:2], mixed[1:number_of // 2 * 2:2]
    slack = jnp.minimum(sizes[donor] - 1, bound - sizes[taker]) // 2
    slack = jnp.where((donor == ranking[0]) | (taker == ranking[0]) | (sizes[taker] == 0), 0, jnp.maximum(slack, 0))
    moved = jax.random.randint(jax.random.fold_in(own, 4), (number_of // 2,), 0, 1 << 20) % (slack + 1)
    sizes = sizes.at[donor].add(-moved).at[taker].add(moved)
    labels = jnp.searchsorted(jnp.cumsum(sizes), jnp.arange(rows * top), side="right").astype(jnp.int32)
    listing = labels.reshape(top, rows).T
    listing = listing[jax.random.permutation(jax.random.fold_in(own, 1), rows)]
    turn = jax.random.randint(jax.random.fold_in(own, 2), (rows, 1), 0, top)
    return jnp.take_along_axis(listing, (jnp.arange(top)[None, :] + turn) % top, axis=1)


def portions_of(number_of, total, bound, skew, full):
    portions = [(1 << 20) // math.isqrt(grade ** skew) + 1 for grade in range(1, number_of + 1)]
    largest = bound if full else min(bound, max(-(-total // number_of), total * portions[0] // sum(portions)))
    least = 1 if total - largest >= number_of - 1 else 0
    holding, spare = [largest] + [least] * (number_of - 1), total - largest - least * (number_of - 1)
    while spare > 0:
        candidates = [i for i in range(1, number_of) if holding[i] < largest] or [i for i in range(1, number_of) if holding[i] < bound]
        mass, budget = sum([portions[i] for i in candidates]), spare
        for i in candidates:
            more = min(bound - holding[i], max(1, budget * portions[i] // mass), spare)
            holding[i] = holding[i] + more
            spare = spare - more
    return np.array(holding)


def setup_inputs(seed: int = 0) -> dict:
    streams_of = jax.random.split(jax.random.key(seed), 5)
    traces = draw_traces(jax.random.fold_in(streams_of[4], 71), 0)
    bin_ids = draw_bin_ids(jax.random.fold_in(streams_of[4], 71), 0)
    valid = with_ends((jax.random.randint(streams_of[2], (TRACES,), 0, 4) < 1).astype(jnp.int32), jax.random.fold_in(streams_of[2], 1), 0, 1)
    tile_owner_keys = jax.random.split(jax.random.fold_in(streams_of[3], 1), TILES // TILES_DEV)
    tile_owner_turns = jax.random.permutation(jax.random.fold_in(streams_of[3], 3), TILES // TILES_DEV)
    tile_owner = jax.vmap(lambda own, number: assign_block(jax.random.fold_in(streams_of[3], 2), own, number, TILES_DEV, N_BINS, 1, CAP, 2))(tile_owner_keys, tile_owner_turns).reshape((TILES, 1))
    return dict(traces=traces, bin_ids=bin_ids, valid=valid, tile_owner=tile_owner)


def time_table(freq_index, times, total):
    phase = (freq_index[None, :] + 1) * times[:, None] % total
    angle = phase.astype(jnp.float32) * (2.0 * math.pi / total)
    norm = 1.0 / math.sqrt(total)
    table = jnp.stack([jnp.cos(angle) * norm, -jnp.sin(angle) * norm], axis=2)
    return table.reshape(times.shape[0], -1).astype(jnp.bfloat16)

def rebuild(observed, coverage):
    state = observed
    for step in range(ITERS):
        mixed = coverage * observed + (1.0 - coverage) * state
        field = (mixed[0] + 1j * mixed[1]).reshape(MX, MY, HX, HY)
        spectrum = jnp.fft.fftn(field)
        power = spectrum.real ** 2 + spectrum.imag ** 2
        damping = 0.5 * jnp.mean(power) + 1e-06
        kept = spectrum * (power / (power + damping))
        back = jnp.fft.ifftn(kept).reshape(-1)
        state = jnp.stack([back.real, back.imag]).astype(jnp.float32)
    return state

def reference(traces, bin_ids, valid, tile_owner):
    cells = MX * MY * HX * HY
    owner = jnp.repeat(tile_owner[:, 0], TILE)
    target = jnp.where(valid > 0, owner * LB + bin_ids, cells).astype(jnp.int32)
    count = jax.ops.segment_sum(jnp.ones(target.shape, jnp.float32), target, cells + 1)[:cells]
    coverage = jnp.minimum(count, 1.0)
    width = NT // N_FREQ
    freq_index = jnp.arange(NF, dtype=jnp.int32)

    def add_block(total, block_no):
        start = (block_no * width).astype(jnp.int32)
        block = lax.dynamic_slice_in_dim(traces, start, width, 0).astype(jnp.float32).T
        sums = jax.ops.segment_sum(block, target, cells + 1)[:cells]
        binned = (sums / jnp.maximum(count, 1.0)[:, None]).astype(jnp.bfloat16)
        times = start + jnp.arange(width, dtype=jnp.int32)
        table = time_table(freq_index, times, NT)
        return (total + jnp.dot(binned, table, preferred_element_type=jnp.float32), None)
    total, unused = lax.scan(add_block, jnp.zeros((cells, 2 * NF), jnp.float32), jnp.arange(N_FREQ, dtype=jnp.int32))
    observed = jnp.transpose(total.reshape(cells, NF, 2), (1, 2, 0))
    return lax.map(lambda slice_obs: rebuild(slice_obs, coverage), observed)
```

```python
import functools
import math

import jax
import jax.numpy as jnp
import numpy as np
from jax import lax
from jax.experimental import pallas as pl
from jax.experimental.pallas import tpu as pltpu
from jax.sharding import PartitionSpec as P

MESH = pl.DeviceIdType.MESH
ITERS = 2
TILE = 128
LB = 1024
YN = 4
XN = 4
CN = 2
NQ = 8
BF_STEPS = 4
NJ = 4
F32 = jnp.float32
BF16 = jnp.bfloat16


def dft_table(zn, samples):
    groups = XN * CN
    total = samples * groups
    x, y, c, z = np.meshgrid(np.arange(XN), np.arange(YN), np.arange(CN), np.arange(zn), indexing="ij")
    freq = (((z * YN + y) * XN + x) * CN + c).reshape(-1)
    phase = ((freq[:, None] + 1) * np.arange(total)[None, :]) % total
    angle = phase.astype(np.float32) * np.float32(2.0 * math.pi / total)
    norm = np.float32(1.0 / math.sqrt(total))
    table = np.stack([np.cos(angle) * norm, -np.sin(angle) * norm], axis=1).astype(BF16)
    rows = table.reshape(2 * freq.size, groups, samples)
    return np.ascontiguousarray(rows.transpose(1, 0, 2))


def spectra_kernel(x_hbm, tab_hbm, lab_hbm, out_hbm, labs_hbm,
                   xm, tab, far_out, far_l, far_r, near_r_out, near_l_out, near_l, near_r, fin,
                   tab_sem, loc_sem, core_send, core_recv, far_send, far_recv, near_send, near_recv,
                   y_send, y_recv, lab_send, lab_recv, own_sem, lab_own):
    bins = lax.axis_index("bins")
    freq = lax.axis_index("freq")
    z, y = bins // YN, bins % YN
    x, c = freq // CN, freq % CN
    nq, chunk = xm.shape[1], xm.shape[3]
    half = nq * chunk
    blk = tab.shape[1] // XN
    part = blk // (YN * CN)
    right = (bins, lax.rem(x + 1, XN) * CN + c)
    left = (bins, lax.rem(x + XN - 1, XN) * CN + c)
    other = (bins, x * CN + (1 - c))

    def plane(dy, dc):
        return (z * YN + lax.rem(y + dy, YN), x * CN + lax.rem(c + dc, CN))

    peers = [(dy, dc) for dy in range(YN) for dc in range(CN) if (dy, dc) != (0, 0)]

    tab_copy = pltpu.make_async_copy(tab_hbm.at[pl.ds(x * CN, CN)], tab, tab_sem)
    tab_copy.start()

    def local_copy(q):
        return pltpu.make_async_copy(
            x_hbm.at[:, pl.ds(pl.multiple_of(c * half + q * chunk, chunk), chunk)], xm.at[c, q], loc_sem.at[q])

    def core_copy(q):
        return pltpu.make_async_remote_copy(
            src_ref=x_hbm.at[:, pl.ds(pl.multiple_of((1 - c) * half + q * chunk, chunk), chunk)], dst_ref=xm.at[c, q],
            send_sem=core_send.at[q], recv_sem=core_recv.at[q], device_id=other, device_id_type=MESH)

    def core_arrival(q):
        return pltpu.make_async_remote_copy(
            src_ref=x_hbm.at[:, pl.ds(pl.multiple_of(c * half + q * chunk, chunk), chunk)], dst_ref=xm.at[1 - c, q],
            send_sem=core_send.at[q], recv_sem=core_recv.at[q], device_id=other, device_id_type=MESH)

    @pl.loop(0, nq)
    def _(q):
        local_copy(q).start()

    barrier = pltpu.get_barrier_semaphore()
    for device in [left, right] + [plane(dy, dc) for dy, dc in peers]:
        pl.semaphore_signal(barrier, inc=1, device_id=device, device_id_type=MESH)
    pl.semaphore_wait(barrier, 2 + len(peers))

    @pl.loop(0, nq)
    def _(q):
        core_copy(q).start()

    def lab_copy(dy):
        return pltpu.make_async_remote_copy(
            src_ref=lab_hbm, dst_ref=labs_hbm.at[y], send_sem=lab_send.at[dy - 1], recv_sem=lab_recv.at[dy - 1],
            device_id=plane(dy, 0), device_id_type=MESH)

    lab_local = pltpu.make_async_copy(lab_hbm, labs_hbm.at[y], lab_own)
    lab_local.start()
    for dy in range(1, YN):
        lab_copy(dy).start()

    def product(dest, q):
        rows = pl.ds(pl.multiple_of(dest * blk, blk), blk)
        first = jnp.dot(tab[0, rows, :], xm[0, q], preferred_element_type=F32)
        return first + jnp.dot(tab[1, rows, :], xm[1, q], preferred_element_type=F32)

    def far_copy(q, side):
        target = right if side == 0 else left
        rows = pl.ds(side * (blk // 2), blk // 2)
        land = far_l if side == 0 else far_r
        return pltpu.make_async_remote_copy(
            src_ref=far_out.at[q, rows], dst_ref=land.at[q], send_sem=far_send.at[side, q],
            recv_sem=far_recv.at[side, q], device_id=target, device_id_type=MESH)

    def near_copy(q, side):
        target = right if side == 0 else left
        source = near_r_out if side == 0 else near_l_out
        land = near_l if side == 0 else near_r
        return pltpu.make_async_remote_copy(
            src_ref=source.at[q], dst_ref=land.at[q], send_sem=near_send.at[side, q],
            recv_sem=near_recv.at[side, q], device_id=target, device_id_type=MESH)

    def y_copy(q, i):
        dy, dc = peers[i]
        to_y, to_c = lax.rem(y + dy, YN), lax.rem(c + dc, CN)
        rows = pl.ds(pl.multiple_of((to_y * CN + to_c) * part, part), part)
        return pltpu.make_async_remote_copy(
            src_ref=fin.at[q, rows], dst_ref=out_hbm.at[y * CN + c, q], send_sem=y_send.at[i, q],
            recv_sem=y_recv.at[i, q], device_id=plane(dy, dc), device_id_type=MESH)

    def own_copy(q):
        rows = pl.ds(pl.multiple_of((y * CN + c) * part, part), part)
        return pltpu.make_async_copy(fin.at[q, rows], out_hbm.at[y * CN + c, q], own_sem.at[q])

    tab_copy.wait()

    @pl.loop(0, nq)
    def _(q):
        local_copy(q).wait()
        core_arrival(q).wait_recv()
        far_out[q] = product(lax.rem(x + 2, XN), q).astype(BF16)
        far_copy(q, 0).start()
        far_copy(q, 1).start()

    @pl.loop(0, nq)
    def _(q):
        to_right = product(lax.rem(x + 1, XN), q)
        to_left = product(lax.rem(x + XN - 1, XN), q)
        far_copy(q, 0).wait_recv()
        near_r_out[q, : blk // 2] = (to_right[: blk // 2] + far_l[q].astype(F32)).astype(BF16)
        near_r_out[q, blk // 2:] = to_right[blk // 2:].astype(BF16)
        near_copy(q, 0).start()
        far_copy(q, 1).wait_recv()
        near_l_out[q, : blk // 2] = to_left[: blk // 2].astype(BF16)
        near_l_out[q, blk // 2:] = (to_left[blk // 2:] + far_r[q].astype(F32)).astype(BF16)
        near_copy(q, 1).start()

    @pl.loop(0, nq)
    def _(q):
        mine = product(x, q)
        near_copy(q, 0).wait_recv()
        near_copy(q, 1).wait_recv()
        fin[q] = (mine + (near_l[q].astype(F32) + near_r[q].astype(F32))).astype(BF16)
        for i in range(len(peers)):
            y_copy(q, i).start()
        own_copy(q).start()

    @pl.loop(0, nq)
    def _(q):
        core_copy(q).wait_send()
        for side in (0, 1):
            far_copy(q, side).wait_send()
            near_copy(q, side).wait_send()
        for i in range(len(peers)):
            y_copy(q, i).wait()
        own_copy(q).wait()

    for dy in range(1, YN):
        lab_copy(dy).wait()
    lab_local.wait()


def spectra(traces, table, labels):
    samples, width = traces.shape
    groups, rows, _ = table.shape
    half = width // CN
    nq = min(NQ, half // 512)
    chunk = half // nq
    blk = rows // XN
    part = blk // (YN * CN)
    dma = pltpu.SemaphoreType.DMA
    npeer = YN * CN - 1
    any_spec = pl.BlockSpec(memory_space=pl.ANY)
    return pl.pallas_call(
        spectra_kernel,
        out_shape=(
            jax.ShapeDtypeStruct((YN * CN, nq, part, chunk), BF16),
            jax.ShapeDtypeStruct((YN,) + labels.shape, jnp.int32),
        ),
        in_specs=[any_spec] * 3,
        out_specs=(any_spec, any_spec),
        scratch_shapes=[
            pltpu.VMEM((CN, nq, samples, chunk), BF16),
            pltpu.VMEM((CN, rows, samples), BF16),
            pltpu.VMEM((nq, blk, chunk), BF16),
            pltpu.VMEM((nq, blk // 2, chunk), BF16),
            pltpu.VMEM((nq, blk // 2, chunk), BF16),
            pltpu.VMEM((nq, blk, chunk), BF16),
            pltpu.VMEM((nq, blk, chunk), BF16),
            pltpu.VMEM((nq, blk, chunk), BF16),
            pltpu.VMEM((nq, blk, chunk), BF16),
            pltpu.VMEM((nq, blk, chunk), BF16),
            dma, dma((nq,)), dma((nq,)), dma((nq,)), dma((2, nq)), dma((2, nq)), dma((2, nq)), dma((2, nq)),
            dma((npeer, nq)), dma((npeer, nq)), dma((YN - 1,)), dma((YN - 1,)), dma((nq,)), dma,
        ],
        compiler_params=pltpu.CompilerParams(
            collective_id=0, has_side_effects=True, vmem_limit_bytes=56 * 1024 * 1024),
        cost_estimate=pl.CostEstimate(flops=2 * rows * samples * width, bytes_accessed=12 << 20, transcendentals=0),
        name="spectra",
    )(traces, table, labels)


def bin_kernel(own_ref, val_ref, lab_ref, acc_ref, cnt_ref):
    step = pl.program_id(0)
    _, nq, part, chunk = val_ref.shape
    per = chunk // TILE

    @pl.when(step == 0)
    def _():
        acc_ref[...] = jnp.zeros_like(acc_ref)
        cnt_ref[...] = jnp.zeros_like(cnt_ref)

    high = lax.broadcasted_iota(jnp.int32, (LB // TILE, TILE), 0)
    low = lax.broadcasted_iota(jnp.int32, (TILE, TILE), 0)

    @pl.loop(0, nq)
    def _(q):
        for r in range(per):
            tile = step * (nq * per) + q * per + r
            label = lab_ref[pl.ds(q * per + r, 1), :] & 2047
            vals = val_ref[0, q, :, r * TILE:(r + 1) * TILE].astype(F32)
            hot_high = (label // TILE == high).astype(F32)
            hot_low = ((label & (TILE - 1)) == low).astype(F32).astype(BF16)
            spread = (vals[:, None, :] * hot_high[None]).reshape(part * (LB // TILE), TILE)
            left = jnp.concatenate([spread, hot_high], axis=0).astype(BF16)
            sums = lax.dot_general(left, hot_low, (((1,), (1,)), ((), ())), preferred_element_type=F32)
            rows = pl.ds(pl.multiple_of(own_ref[tile] * (LB // TILE), LB // TILE), LB // TILE)
            acc_ref[:, rows, :] += sums[: part * (LB // TILE)].reshape(part, LB // TILE, TILE)
            cnt_ref[rows, :] += sums[part * (LB // TILE):]


def bin_plane(owners, vals, labels, n_owners):
    src, nq, part, chunk = vals.shape
    tiles = labels.shape[0]
    rows = n_owners * (LB // TILE)
    return pl.pallas_call(
        bin_kernel,
        grid_spec=pltpu.PrefetchScalarGridSpec(
            num_scalar_prefetch=1,
            grid=(src,),
            in_specs=[
                pl.BlockSpec((1, nq, part, chunk), lambda i, own: (i, 0, 0, 0)),
                pl.BlockSpec((tiles // src, TILE), lambda i, own: (i, 0)),
            ],
            out_specs=[
                pl.BlockSpec((part, rows, TILE), lambda i, own: (0, 0, 0)),
                pl.BlockSpec((rows, TILE), lambda i, own: (0, 0)),
            ],
        ),
        out_shape=(
            jax.ShapeDtypeStruct((part, rows, TILE), F32),
            jax.ShapeDtypeStruct((rows, TILE), F32),
        ),
        compiler_params=pltpu.CompilerParams(vmem_limit_bytes=56 * 1024 * 1024),
        name="bin_plane",
    )(owners, vals, labels)


def reduce_kernel(zn, bf_steps, acc_hbm, cnt_hbm, out_ref, tot_ref,
                  own, rb, sb, rf, sf, cz,
                  own_sem, b_send, b_recv, f_send, f_recv, cz_own, cz_send, cz_recv, g_send, g_recv):
    bins = lax.axis_index("bins")
    freq = lax.axis_index("freq")
    z, y = bins // YN, bins % YN
    x, c = freq // CN, freq % CN
    hops = zn // 2
    nj = NJ
    crow = cz.shape[1]
    rows = own.shape[2]
    place = (y * XN + x) * CN + c

    def along_z(dz):
        return (lax.rem(z + dz, zn) * YN + y, freq)

    nexts = (along_z(1), along_z(zn - 1))
    x_peer = [(bins, lax.rem(x + dx, XN) * CN + c) for dx in range(1, XN)]
    y_peer = [(z * YN + lax.rem(y + dy, YN), freq) for dy in range(1, YN)]
    c_peer = (bins, x * CN + 1 - c)

    def dest_of(slot):
        if slot == 0:
            return lax.rem(z + hops, zn)
        if slot < hops:
            return lax.rem(z + hops - slot, zn)
        if slot < 2 * hops - 1:
            return lax.rem(z + hops + (slot - hops + 1), zn)
        return z

    order = [0]
    for s in range(1, hops):
        order += [s, hops - 1 + s]
    order += [2 * hops - 1]

    def own_copy(slot):
        return pltpu.make_async_copy(acc_hbm.at[pl.ds(dest_of(slot) * 2, 2)], own.at[slot], own_sem.at[slot])

    for slot in order:
        own_copy(slot).start()
    mine = pl.ds(pl.multiple_of(place * crow, crow), crow)
    cnt_own = pltpu.make_async_copy(cnt_hbm.at[mine], cz.at[z], cz_own)
    cnt_own.start()

    barrier = pltpu.get_barrier_semaphore()

    @pl.loop(1, zn)
    def _(dz):
        pl.semaphore_signal(barrier, inc=1, device_id=along_z(dz), device_id_type=MESH)

    for device in x_peer + y_peer + [c_peer]:
        pl.semaphore_signal(barrier, inc=1, device_id=device, device_id_type=MESH)
    pl.semaphore_wait(barrier, zn - 1 + len(x_peer) + len(y_peer) + 1)

    def cz_copy(dz):
        return pltpu.make_async_remote_copy(
            src_ref=cnt_hbm.at[mine], dst_ref=cz.at[z], send_sem=cz_send.at[dz - 1], recv_sem=cz_recv.at[dz - 1],
            device_id=along_z(dz), device_id_type=MESH)

    def b_copy(side, s, j):
        return pltpu.make_async_remote_copy(
            src_ref=sb.at[side, s, j], dst_ref=rb.at[side, s, j], send_sem=b_send.at[side, s, j],
            recv_sem=b_recv.at[side, s, j], device_id=nexts[side], device_id_type=MESH)

    def f_copy(side, s, j):
        return pltpu.make_async_remote_copy(
            src_ref=sf.at[side, s - bf_steps, j], dst_ref=rf.at[side, s - bf_steps, j],
            send_sem=f_send.at[side, s - bf_steps, j],
            recv_sem=f_recv.at[side, s - bf_steps, j], device_id=nexts[side], device_id_type=MESH)

    per = rows * 2 // nj

    def own_piece(slot, j):
        first = j * per // rows
        return own[slot, first, (j * per) % rows:(j * per) % rows + per, :]

    own_copy(0).wait()
    for j in range(nj):
        side = 0 if j < nj // 2 else 1
        sb[side, 0, j] = own_piece(0, j).astype(BF16)
        b_copy(side, 0, j).start()

    @pl.loop(1, zn)
    def _(dz):
        cz_copy(dz).start()

    for s in range(1, hops):
        for side in (0, 1):
            slot = s if side == 0 else hops - 1 + s
            own_copy(slot).wait()
        for j in range(nj):
            for side in (0, 1):
                slot = s if side == 0 else hops - 1 + s
                piece = own_piece(slot, j)
                if s - 1 >= bf_steps:
                    f_copy(side, s - 1, j).wait_recv()
                    piece = piece + rf[side, s - 1 - bf_steps, j]
                elif s - 1 > 0 or (side == 0) == (j < nj // 2):
                    b_copy(side, s - 1, j).wait_recv()
                    piece = piece + rb[side, s - 1, j].astype(F32)
                if s < bf_steps:
                    sb[side, s, j] = piece.astype(BF16)
                    b_copy(side, s, j).start()
                else:
                    sf[side, s - bf_steps, j] = piece
                    f_copy(side, s, j).start()
        if s == 1:
            @pl.loop(1, zn)
            def _(dz):
                cz_copy(dz).wait()
            cnt_own.wait()
            tot_ref[pl.ds(place, 1)] = jnp.sum(cz[...], axis=0)[None]

        def gather(i, size, device):
            first = place // size * size
            part = pl.ds(first, size)
            return pltpu.make_async_remote_copy(
                src_ref=tot_ref.at[part], dst_ref=tot_ref.at[part], send_sem=g_send.at[i], recv_sem=g_recv.at[i],
                device_id=device, device_id_type=MESH)

        stages = [
            [(0, 1, c_peer)],
            [(1 + i, CN, device) for i, device in enumerate(x_peer)],
            [(XN + i, CN * XN, device) for i, device in enumerate(y_peer)],
        ]
        first_stage = max(1, hops - 5)
        for n, stage in enumerate(stages):
            if s == min(hops - 1, first_stage + n):
                if n:
                    for args in stages[n - 1]:
                        gather(*args).wait()
                for args in stage:
                    gather(*args).start()
        if s == hops - 1:
            for args in stages[-1]:
                gather(*args).wait()

    last = 2 * hops - 1
    own_copy(last).wait()
    for j in range(nj):
        for side in (0, 1):
            if hops > bf_steps:
                f_copy(side, hops - 1, j).wait_recv()
            else:
                b_copy(side, hops - 1, j).wait_recv()
        if hops > bf_steps:
            arrived = rf[0, hops - 1 - bf_steps, j] + rf[1, hops - 1 - bf_steps, j]
        else:
            arrived = rb[0, hops - 1, j].astype(F32) + rb[1, hops - 1, j].astype(F32)
        first = j * per // rows
        out_ref[first, (j * per) % rows:(j * per) % rows + per, :] = arrived + own_piece(last, j)

    for s in range(hops):
        for j in range(nj):
            for side in (0, 1):
                if s == 0 and (side == 0) != (j < nj // 2):
                    continue
                if s < bf_steps:
                    b_copy(side, s, j).wait_send()
                else:
                    f_copy(side, s, j).wait_send()


def reduce_planes(acc, cnt, zn):
    part, rows, _ = acc.shape
    hops = zn // 2
    bf = min(BF_STEPS, hops)
    fs = max(hops - bf, 1)
    per = rows * 2 // NJ
    places = YN * XN * CN
    crow = rows // places
    dma = pltpu.SemaphoreType.DMA
    any_spec = pl.BlockSpec(memory_space=pl.ANY)
    return pl.pallas_call(
        functools.partial(reduce_kernel, zn, bf),
        out_shape=(
            jax.ShapeDtypeStruct((2, rows, TILE), F32),
            jax.ShapeDtypeStruct((places, crow, TILE), F32),
        ),
        in_specs=[any_spec, any_spec],
        out_specs=(pl.BlockSpec(memory_space=pltpu.VMEM), pl.BlockSpec(memory_space=pltpu.VMEM)),
        scratch_shapes=[
            pltpu.VMEM((zn, 2, rows, TILE), F32),
            pltpu.VMEM((2, bf, NJ, per, TILE), BF16),
            pltpu.VMEM((2, bf, NJ, per, TILE), BF16),
            pltpu.VMEM((2, fs, NJ, per, TILE), F32),
            pltpu.VMEM((2, fs, NJ, per, TILE), F32),
            pltpu.VMEM((zn, crow, TILE), F32),
            dma((zn,)), dma((2, bf, NJ)), dma((2, bf, NJ)), dma((2, fs, NJ)), dma((2, fs, NJ)),
            dma, dma((zn - 1,)), dma((zn - 1,)), dma((7,)), dma((7,)),
        ],
        compiler_params=pltpu.CompilerParams(
            collective_id=1, has_side_effects=True, vmem_limit_bytes=56 * 1024 * 1024),
        cost_estimate=pl.CostEstimate(flops=0, bytes_accessed=12 << 20, transcendentals=0),
        name="reduce_planes",
    )(acc, cnt)


def grid_tables():
    index = np.arange(256)
    a, b = index // 16, index % 16
    phase = (a[:, None] * a[None, :] + b[:, None] * b[None, :]) % 16
    angle = 2.0 * np.pi * phase / 16.0
    cos, sin = np.cos(angle), np.sin(angle)
    forward = np.block([[cos, sin], [-sin, cos]]).astype(np.float32)
    inverse = np.block([[cos, -sin], [sin, cos]]).astype(np.float32)
    both = []
    for m in (forward, inverse):
        hi = m.astype(BF16)
        lo = (m - hi.astype(np.float32)).astype(BF16)
        both.append(np.stack([hi, lo]))
    return np.stack(both)


def split(value):
    hi = value.astype(BF16)
    return hi, (value - hi.astype(F32)).astype(BF16)


def mwni_kernel(sum_ref, cnt_ref, tab_ref, out_ref):
    n = 256

    def grid(ref):
        return jnp.concatenate([ref[pl.ds(0, n, stride=2), :], ref[pl.ds(1, n, stride=2), :]], axis=1)

    def left_dot(m, value):
        hi, lo = split(value)
        t_hi, t_lo = tab_ref[m, 0], tab_ref[m, 1]
        dot = functools.partial(jnp.dot, preferred_element_type=F32)
        return dot(t_hi, hi) + (dot(t_hi, lo) + dot(t_lo, hi))

    def right_dot(m, value):
        hi, lo = split(value)
        t_hi, t_lo = tab_ref[m, 0], tab_ref[m, 1]
        dot = functools.partial(jnp.dot, preferred_element_type=F32)
        return dot(hi, t_hi) + (dot(lo, t_hi) + dot(hi, t_lo))

    def transform(forward, re, im):
        mid = left_dot(0 if forward else 1, jnp.concatenate([re, im], axis=0))
        out = right_dot(1 if forward else 0, jnp.concatenate([mid[:n], mid[n:]], axis=1))
        return out[:, :n], out[:, n:]

    count = grid(cnt_ref)
    cover = jnp.minimum(count, 1.0)
    scale = 1.0 / jnp.maximum(count, 1.0)
    obs_re = grid(sum_ref.at[0]) * scale
    obs_im = grid(sum_ref.at[1]) * scale
    re, im = obs_re, obs_im
    cells = n * n
    for step in range(ITERS):
        u_re = cover * obs_re + (1.0 - cover) * re
        u_im = cover * obs_im + (1.0 - cover) * im
        f_re, f_im = transform(True, u_re, u_im)
        power = f_re * f_re + f_im * f_im
        lam = 0.5 * (jnp.sum(power) / cells) + 1e-06
        keep = power / (power + lam)
        re, im = transform(False, f_re * keep, f_im * keep)
        re, im = re * (1.0 / cells), im * (1.0 / cells)
    out_ref[0] = re
    out_ref[1] = im


def mwni(sums, counts, tables):
    vmem = pl.BlockSpec(memory_space=pltpu.VMEM)
    return pl.pallas_call(
        mwni_kernel,
        out_shape=jax.ShapeDtypeStruct((2, 256, 256), F32),
        in_specs=[vmem] * 3,
        out_specs=vmem,
        compiler_params=pltpu.CompilerParams(vmem_limit_bytes=56 * 1024 * 1024),
        name="mwni",
    )(sums, counts, tables)


def local(zn, table, tables, traces, bin_ids, valid, tile_owner):
    n_owners = zn * YN
    tiles = tile_owner.shape[0]
    labels = jnp.where(valid > 0, bin_ids, LB).reshape(tiles, TILE) + tile_owner * 2048
    vals, labs = spectra(traces, table, labels)
    labs = labs.reshape(YN * tiles, TILE)
    owners = labs[:, 0] // 2048
    acc, cnt = bin_plane(owners, vals, labs, n_owners)
    sums, counts = reduce_planes(acc, cnt, zn)
    state = mwni(sums, counts.reshape(-1, TILE), tables)
    return state.reshape(1, 2, -1)


def solution(mesh):
    zn = mesh.shape["bins"] // YN
    table = dft_table(zn, 250)
    tables = grid_tables()
    in_specs = (P("freq", "bins"), P("bins"), P("bins"), P("bins", None))
    out_specs = P(("bins", "freq"), None, None)

    def run(traces, bin_ids, valid, tile_owner):
        return jax.shard_map(
            functools.partial(local, zn, jnp.asarray(table), jnp.asarray(tables)),
            mesh=mesh, in_specs=in_specs, out_specs=out_specs, check_vma=False,
        )(traces, bin_ids, valid, tile_owner)

    return run
```

```python
import functools
import math

import jax
import jax.numpy as jnp
import numpy as np
from jax import lax
from jax.experimental import pallas as pl
from jax.experimental.pallas import tpu as pltpu
from jax.sharding import PartitionSpec as P

MESH = pl.DeviceIdType.MESH
ITERS = 2
TILE = 128
LB = 1024
YN = 4
XN = 4
CN = 2
NQ = 8
BF_STEPS = 6
NJ = 4
F32 = jnp.float32
BF16 = jnp.bfloat16


def dft_table(zn, samples):
    groups = XN * CN
    total = samples * groups
    x, y, c, z = np.meshgrid(np.arange(XN), np.arange(YN), np.arange(CN), np.arange(zn), indexing="ij")
    freq = (((z * YN + y) * XN + x) * CN + c).reshape(-1)
    phase = ((freq[:, None] + 1) * np.arange(total)[None, :]) % total
    angle = phase.astype(np.float32) * np.float32(2.0 * math.pi / total)
    norm = np.float32(1.0 / math.sqrt(total))
    table = np.stack([np.cos(angle) * norm, -np.sin(angle) * norm], axis=0).astype(BF16)
    rows = table.reshape(2 * freq.size, groups, samples)
    return np.ascontiguousarray(rows.transpose(1, 0, 2))


HIGH = LB // TILE


def observe_kernel(zn, x_hbm, tab_hbm, ids_ref, valid_ref, owner_ref, out_ref, tot_ref,
                   xm, tab, far_out, far_l, far_r, near_r_out, near_l_out, near_l, near_r, fin,
                   plane0, plane1, acc0, acc1, cnt, pay, labs, slots, rb, sb, rf, sf, cz,
                   tab_sem, loc_sem, core_send, core_recv, far_send, far_recv, near_send, near_recv,
                   y_send, y_recv, own_sem, lab_send, lab_recv, lab_own, slot_sem,
                   b_send, b_recv, f_send, f_recv, cz_own, cz_send, cz_recv, g_send, g_recv):
    bins = lax.axis_index("bins")
    freq = lax.axis_index("freq")
    z, y = bins // YN, bins % YN
    x, c = freq // CN, freq % CN
    nq, chunk = xm.shape[1], xm.shape[3]
    per_chunk = chunk // TILE
    half = nq * chunk
    blk = tab.shape[1] // XN // 2
    part = blk // (YN * CN)
    tiles = ids_ref.shape[0]
    hops = zn // 2
    rows = acc0.shape[1]
    nj = NJ
    per = rows // nj
    crow = cz.shape[1]
    place = (y * XN + x) * CN + c
    spectra, accs = (plane0, plane1), (acc0, acc1)

    right = (bins, lax.rem(x + 1, XN) * CN + c)
    left = (bins, lax.rem(x + XN - 1, XN) * CN + c)
    other = (bins, x * CN + (1 - c))

    def plane(dy, dc):
        return (z * YN + lax.rem(y + dy, YN), x * CN + lax.rem(c + dc, CN))

    def along_z(dz):
        return (lax.rem(z + dz, zn) * YN + y, freq)

    nexts = (along_z(1), along_z(zn - 1))
    peers = [(dy, dc) for dy in range(YN) for dc in range(CN) if (dy, dc) != (0, 0)]
    x_peer = [(bins, lax.rem(x + dx, XN) * CN + c) for dx in range(1, XN)]
    y_peer = [plane(dy, 0) for dy in range(1, YN)]

    def remote(src, dst, send, recv, device):
        return pltpu.make_async_remote_copy(
            src_ref=src, dst_ref=dst, send_sem=send, recv_sem=recv, device_id=device, device_id_type=MESH)

    tab_copy = pltpu.make_async_copy(tab_hbm.at[pl.ds(x * CN, CN)], tab, tab_sem)
    tab_copy.start()

    def piece_of(side, q):
        return x_hbm.at[:, pl.ds(pl.multiple_of(side * half + q * chunk, chunk), chunk)]

    def local_copy(q):
        return pltpu.make_async_copy(piece_of(c, q), xm.at[c, q], loc_sem.at[q])

    def core_copy(q):
        return remote(piece_of(1 - c, q), xm.at[c, q], core_send.at[q], core_recv.at[q], other)

    def core_arrival(q):
        return remote(piece_of(c, q), xm.at[1 - c, q], core_send.at[q], core_recv.at[q], other)

    @pl.loop(0, nq)
    def _(q):
        local_copy(q).start()

    barrier = pltpu.get_barrier_semaphore()
    for device in [left, right] + [plane(dy, dc) for dy, dc in peers]:
        pl.semaphore_signal(barrier, inc=1, device_id=device, device_id_type=MESH)
    pl.semaphore_signal(barrier, inc=1, device_id=x_peer[1], device_id_type=MESH)

    @pl.loop(1, zn)
    def _(dz):
        pl.semaphore_signal(barrier, inc=1, device_id=along_z(dz), device_id_type=MESH)

    pay[:tiles] = jnp.where(valid_ref[...] > 0, ids_ref[...], LB)
    tile_no = lax.broadcasted_iota(jnp.int32, (tiles, TILE), 0)
    named = owner_ref[...] == lax.broadcasted_iota(jnp.int32, (tiles, TILE), 1)
    none = tiles + 2
    first = jnp.min(jnp.where(named, tile_no, none), axis=0, keepdims=True)
    second = jnp.max(jnp.where(named, tile_no, -1), axis=0, keepdims=True)
    second = jnp.where(second > first, second, none)
    tail_row = lax.broadcasted_iota(jnp.int32, (8, TILE), 0)
    pay[tiles:tiles + 8] = jnp.where(tail_row == 0, first, jnp.where(tail_row == 1, second, LB))

    pl.semaphore_wait(barrier, 3 + len(peers) + zn - 1)

    @pl.loop(0, nq)
    def _(q):
        core_copy(q).start()

    def lab_copy(dy):
        return remote(pay, labs.at[y], lab_send.at[dy - 1], lab_recv.at[dy - 1], plane(dy, 0))

    lab_local = pltpu.make_async_copy(pay, labs.at[y], lab_own)
    lab_local.start()
    for dy in range(1, YN):
        lab_copy(dy).start()

    def product(h, dest, q):
        block = pl.ds(pl.multiple_of(h * (blk * XN) + dest * blk, blk), blk)
        return (jnp.dot(tab[0, block, :], xm[0, q], preferred_element_type=F32)
                + jnp.dot(tab[1, block, :], xm[1, q], preferred_element_type=F32))

    def far_copy(hq, side):
        target, land = ((right, far_l), (left, far_r))[side]
        return remote(far_out.at[hq, pl.ds(side * (blk // 2), blk // 2)], land.at[hq],
                      far_send.at[side, hq], far_recv.at[side, hq], target)

    def near_copy(hq, side):
        target, source, land = ((right, near_r_out, near_l), (left, near_l_out, near_r))[side]
        return remote(source.at[hq], land.at[hq], near_send.at[side, hq], near_recv.at[side, hq], target)

    def y_copy(h, q, i):
        dy, dc = peers[i]
        block = pl.ds(pl.multiple_of((lax.rem(y + dy, YN) * CN + lax.rem(c + dc, CN)) * part, part), part)
        return remote(fin.at[h * nq + q, :, block], spectra[h].at[(y * CN + c) * nq + q],
                      y_send.at[h, i, q], y_recv.at[h, i, q], plane(dy, dc))

    def own_copy(h, q):
        block = pl.ds(pl.multiple_of((y * CN + c) * part, part), part)
        return pltpu.make_async_copy(
            fin.at[h * nq + q, :, block], spectra[h].at[(y * CN + c) * nq + q], own_sem.at[h, q])

    def far_step(h, q):
        hq = h * nq + q
        far_out[hq] = product(h, lax.rem(x + 2, XN), q).astype(BF16)
        far_copy(hq, 0).start()
        far_copy(hq, 1).start()

    def near_step(h, q):
        hq = h * nq + q
        to_right = product(h, lax.rem(x + 1, XN), q)
        to_left = product(h, lax.rem(x + XN - 1, XN), q)
        mid = blk // 2
        far_copy(hq, 0).wait_recv()
        near_r_out[hq, :mid] = (to_right[:mid] + far_l[hq].astype(F32)).astype(BF16)
        near_r_out[hq, mid:] = to_right[mid:].astype(BF16)
        near_copy(hq, 0).start()
        far_copy(hq, 1).wait_recv()
        near_l_out[hq, :mid] = to_left[:mid].astype(BF16)
        near_l_out[hq, mid:] = (to_left[mid:] + far_r[hq].astype(F32)).astype(BF16)
        near_copy(hq, 1).start()

    def final_step(h, q):
        hq = h * nq + q
        mine = product(h, x, q)
        near_copy(hq, 0).wait_recv()
        near_copy(hq, 1).wait_recv()
        full = (mine + (near_l[hq].astype(F32) + near_r[hq].astype(F32))).astype(BF16)
        for r in range(per_chunk):
            fin[hq, r] = full[:, r * TILE:(r + 1) * TILE]
        for i in range(len(peers)):
            y_copy(h, q, i).start()
        own_copy(h, q).start()

    low_iota = [(lax.broadcasted_iota(jnp.int32, (16, TILE), 0) + 16 * i).astype(F32).astype(BF16)
                for i in range(TILE // 16)]
    one, zero = jnp.ones((16, TILE), BF16), jnp.zeros((16, TILE), BF16)

    def bin_owner(h, o):
        lefts, rights = [], []
        for yy in range(YN):
            for rank in range(2):
                t = slots[yy, rank, o]
                label = labs[yy, pl.ds(t, 1), :]
                tv = jnp.minimum(t, tiles - 1)
                vals = spectra[h][yy * (tiles // per_chunk) + tv // per_chunk, tv % per_chunk]
                low = jnp.broadcast_to((label & (TILE - 1)).astype(F32), (16, TILE)).astype(BF16)
                high = jnp.broadcast_to((label // TILE).astype(F32), (16, TILE)).astype(BF16)
                pieces = [jnp.where(high == jnp.asarray(k, BF16), vals, zero) for k in range(HIGH)]
                if h == 0:
                    pieces.append(jnp.where(high == low_iota[0], one, zero))
                lefts.append(jnp.concatenate(pieces, axis=0))
                rights.append(jnp.concatenate([jnp.where(low == it, one, zero) for it in low_iota], axis=0))
        sums = lax.dot_general(jnp.concatenate(lefts, axis=1), jnp.concatenate(rights, axis=1),
                               (((1,), (1,)), ((), ())), preferred_element_type=F32)
        where = pl.ds(pl.multiple_of(o * HIGH, HIGH), HIGH)
        accs[h][:, where, :] = jnp.swapaxes(sums[: HIGH * part].reshape(HIGH, part, TILE), 0, 1)
        if h == 0:
            cnt[where, :] = sums[HIGH * part: HIGH * part + HIGH]

    def bin_range(h, j):
        owners = per // HIGH

        @pl.loop(j * owners, (j + 1) * owners)
        def _(o):
            bin_owner(h, o)

    def b_copy(h, side, s, j):
        return remote(sb.at[h, side, s, j], rb.at[h, side, s, j],
                      b_send.at[h, side, s, j], b_recv.at[h, side, s, j], nexts[side])

    def f_copy(h, side, s, j):
        k = s - BF_STEPS
        return remote(sf.at[h, side, k, j], rf.at[h, side, k, j],
                      f_send.at[h, side, k, j], f_recv.at[h, side, k, j], nexts[side])

    def z_send(h, side, s, j, value):
        if s < BF_STEPS:
            sb[h, side, s, j] = value.astype(BF16)
            b_copy(h, side, s, j).start()
        else:
            sf[h, side, s - BF_STEPS, j] = value
            f_copy(h, side, s, j).start()

    def z_take(h, side, s, j):
        if s < BF_STEPS:
            b_copy(h, side, s, j).wait_recv()
            return rb[h, side, s, j].astype(F32)
        f_copy(h, side, s, j).wait_recv()
        return rf[h, side, s - BF_STEPS, j]

    def first_side(j):
        return 0 if j < nj // 2 else 1

    def z_item(h, s, j):
        span = slice(j * per, (j + 1) * per)
        if s == 0:
            bin_range(h, j)
            z_send(h, first_side(j), 0, j, accs[h][lax.rem(z + hops, zn), span, :])
        elif s < hops:
            for side in (0, 1):
                dest = lax.rem(z + hops - s, zn) if side == 0 else lax.rem(z + zn - hops + s, zn)
                value = accs[h][dest, span, :]
                if s > 1 or side == first_side(j):
                    value = value + z_take(h, side, s - 1, j)
                z_send(h, side, s, j, value)
        else:
            value = z_take(h, 0, hops - 1, j) + z_take(h, 1, hops - 1, j)
            out_ref[h, span, :] = value + accs[h][z, span, :]

    mine_rows = pl.ds(pl.multiple_of(place * crow, crow), crow)

    def cz_copy(dz):
        return remote(cnt.at[mine_rows], cz.at[z], cz_send.at[dz - 1], cz_recv.at[dz - 1], along_z(dz))

    cnt_own = pltpu.make_async_copy(cnt.at[mine_rows], cz.at[z], cz_own)

    def gather(i, size, device):
        part_of = pl.ds(place // size * size, size)
        return remote(tot_ref.at[part_of], tot_ref.at[part_of], g_send.at[i], g_recv.at[i], device)

    stages = [
        [(0, 1, other)],
        [(1 + i, CN, device) for i, device in enumerate(x_peer)],
        [(XN + i, CN * XN, device) for i, device in enumerate(y_peer)],
    ]

    tab_copy.wait()

    @pl.loop(0, nq)
    def _(q):
        local_copy(q).wait()
        core_arrival(q).wait_recv()
        far_step(0, q)

    @pl.loop(0, nq)
    def _(q):
        near_step(0, q)

    @pl.loop(0, nq)
    def _(q):
        final_step(0, q)
        far_step(1, q)

    for dy in range(1, YN):
        lab_copy(dy).wait()
    lab_local.wait()
    slot_copy = pltpu.make_async_copy(labs.at[:, pl.ds(tiles, 8)], slots, slot_sem)
    slot_copy.start()
    slot_copy.wait()

    def plane_arrived(h):
        @pl.loop(0, nq)
        def _(q):
            for i in range(len(peers)):
                y_copy(h, q, i).wait_recv()
            own_copy(h, q).wait()

    plane_arrived(0)
    lag = hops
    pair = max(1, nq // 4)
    near_at, final_at = 2, 5
    for d in range(lag + hops + nj):
        for j in range(nj):
            if 0 <= d - j <= hops:
                z_item(0, d - j, j)
        if near_at <= d < near_at + nq // pair:
            @pl.loop((d - near_at) * pair, (d - near_at + 1) * pair)
            def _(q):
                near_step(1, q)
        if final_at <= d < final_at + nq // pair:
            @pl.loop((d - final_at) * pair, (d - final_at + 1) * pair)
            def _(q):
                final_step(1, q)
        if d == lag:
            plane_arrived(1)
        for j in range(nj):
            if 0 <= d - lag - j <= hops:
                z_item(1, d - lag - j, j)
        if d == nj:
            cnt_own.start()

            @pl.loop(1, zn)
            def _(dz):
                cz_copy(dz).start()
        if d == nj + 3:
            @pl.loop(1, zn)
            def _(dz):
                cz_copy(dz).wait()
            cnt_own.wait()
            tot_ref[pl.ds(place, 1)] = jnp.sum(cz[...], axis=0)[None]
            for args in stages[0]:
                gather(*args).start()
        if d == nj + 5:
            for args in stages[0]:
                gather(*args).wait()
            for args in stages[1]:
                gather(*args).start()
        if d == nj + 7:
            for args in stages[1]:
                gather(*args).wait()
            for args in stages[2]:
                gather(*args).start()

    for args in stages[2]:
        gather(*args).wait()

    @pl.loop(0, nq)
    def _(q):
        core_copy(q).wait_send()
        for h in (0, 1):
            for side in (0, 1):
                far_copy(h * nq + q, side).wait_send()
                near_copy(h * nq + q, side).wait_send()
            for i in range(len(peers)):
                y_copy(h, q, i).wait_send()

    for h in (0, 1):
        for s in range(hops):
            for j in range(nj):
                for side in (0, 1):
                    if s == 0 and side != first_side(j):
                        continue
                    if s < BF_STEPS:
                        b_copy(h, side, s, j).wait_send()
                    else:
                        f_copy(h, side, s, j).wait_send()


def observe(zn, traces, table, ids, valid, owner):
    samples, width = traces.shape
    _, table_rows, _ = table.shape
    half = width // CN
    nq = NQ
    chunk = half // nq
    blk = table_rows // XN // 2
    part = blk // (YN * CN)
    tiles = ids.shape[0]
    hops = zn // 2
    fs = hops - BF_STEPS
    rows = zn * YN * HIGH
    per = rows // NJ
    places = YN * XN * CN
    crow = rows // places
    npeer = YN * CN - 1
    dma = pltpu.SemaphoreType.DMA
    any_spec = pl.BlockSpec(memory_space=pl.ANY)
    vmem = pl.BlockSpec(memory_space=pltpu.VMEM)
    plane_buf = pltpu.VMEM((YN * CN * nq, chunk // TILE, part, TILE), BF16)
    return pl.pallas_call(
        functools.partial(observe_kernel, zn),
        out_shape=(
            jax.ShapeDtypeStruct((2, rows, TILE), F32),
            jax.ShapeDtypeStruct((places, crow, TILE), F32),
        ),
        in_specs=[any_spec, any_spec, vmem, vmem, vmem],
        out_specs=(vmem, vmem),
        scratch_shapes=[
            pltpu.VMEM((CN, nq, samples, chunk), BF16),
            pltpu.VMEM((CN, table_rows, samples), BF16),
            pltpu.VMEM((2 * nq, blk, chunk), BF16),
            pltpu.VMEM((2 * nq, blk // 2, chunk), BF16),
            pltpu.VMEM((2 * nq, blk // 2, chunk), BF16),
            pltpu.VMEM((2 * nq, blk, chunk), BF16),
            pltpu.VMEM((2 * nq, blk, chunk), BF16),
            pltpu.VMEM((2 * nq, blk, chunk), BF16),
            pltpu.VMEM((2 * nq, blk, chunk), BF16),
            pltpu.VMEM((2 * nq, chunk // TILE, blk, TILE), BF16),
            plane_buf, plane_buf,
            pltpu.VMEM((part, rows, TILE), F32),
            pltpu.VMEM((part, rows, TILE), F32),
            pltpu.VMEM((rows, TILE), F32),
            pltpu.VMEM((tiles + 8, TILE), jnp.int32),
            pltpu.VMEM((YN, tiles + 8, TILE), jnp.int32),
            pltpu.SMEM((YN, 8, TILE), jnp.int32),
            pltpu.VMEM((2, 2, BF_STEPS, NJ, per, TILE), BF16),
            pltpu.VMEM((2, 2, BF_STEPS, NJ, per, TILE), BF16),
            pltpu.VMEM((2, 2, fs, NJ, per, TILE), F32),
            pltpu.VMEM((2, 2, fs, NJ, per, TILE), F32),
            pltpu.VMEM((zn, crow, TILE), F32),
            dma, dma((nq,)), dma((nq,)), dma((nq,)),
            dma((2, 2 * nq)), dma((2, 2 * nq)), dma((2, 2 * nq)), dma((2, 2 * nq)),
            dma((2, npeer, nq)), dma((2, npeer, nq)), dma((2, nq)),
            dma((YN - 1,)), dma((YN - 1,)), dma, dma,
            dma((2, 2, BF_STEPS, NJ)), dma((2, 2, BF_STEPS, NJ)), dma((2, 2, fs, NJ)), dma((2, 2, fs, NJ)),
            dma, dma((zn - 1,)), dma((zn - 1,)), dma((7,)), dma((7,)),
        ],
        compiler_params=pltpu.CompilerParams(
            collective_id=0, has_side_effects=True, vmem_limit_bytes=60 * 1024 * 1024),
        cost_estimate=pl.CostEstimate(flops=2 * table_rows * samples * width, bytes_accessed=12 << 20, transcendentals=0),
        name="observe",
    )(traces, table, ids, valid, owner)


def grid_tables():
    index = np.arange(256)
    a, b = index // 16, index % 16
    phase = (a[:, None] * a[None, :] + b[:, None] * b[None, :]) % 16
    angle = 2.0 * np.pi * phase / 16.0
    cos, sin = np.cos(angle), np.sin(angle)
    forward = np.block([[cos, sin], [-sin, cos]]).astype(np.float32)
    inverse = np.block([[cos, -sin], [sin, cos]]).astype(np.float32)
    both = []
    for m in (forward, inverse):
        hi = m.astype(BF16)
        lo = (m - hi.astype(np.float32)).astype(BF16)
        both.append(np.stack([hi, lo]))
    return np.stack(both)


def split(value):
    hi = value.astype(BF16)
    return hi, (value - hi.astype(F32)).astype(BF16)


def mwni_kernel(sum_ref, cnt_ref, tab_ref, out_ref):
    n = 256

    def grid(ref):
        return jnp.concatenate([ref[pl.ds(0, n, stride=2), :], ref[pl.ds(1, n, stride=2), :]], axis=1)

    def left_dot(m, value):
        hi, lo = split(value)
        t_hi, t_lo = tab_ref[m, 0], tab_ref[m, 1]
        dot = functools.partial(jnp.dot, preferred_element_type=F32)
        return dot(t_hi, hi) + (dot(t_hi, lo) + dot(t_lo, hi))

    def right_dot(m, value):
        hi, lo = split(value)
        t_hi, t_lo = tab_ref[m, 0], tab_ref[m, 1]
        dot = functools.partial(jnp.dot, preferred_element_type=F32)
        return dot(hi, t_hi) + (dot(lo, t_hi) + dot(hi, t_lo))

    def transform(forward, re, im):
        mid = left_dot(0 if forward else 1, jnp.concatenate([re, im], axis=0))
        out = right_dot(1 if forward else 0, jnp.concatenate([mid[:n], mid[n:]], axis=1))
        return out[:, :n], out[:, n:]

    count = grid(cnt_ref)
    cover = jnp.minimum(count, 1.0)
    scale = 1.0 / jnp.maximum(count, 1.0)
    obs_re = grid(sum_ref.at[0]) * scale
    obs_im = grid(sum_ref.at[1]) * scale
    re, im = obs_re, obs_im
    cells = n * n
    for step in range(ITERS):
        u_re = cover * obs_re + (1.0 - cover) * re
        u_im = cover * obs_im + (1.0 - cover) * im
        f_re, f_im = transform(True, u_re, u_im)
        power = f_re * f_re + f_im * f_im
        lam = 0.5 * (jnp.sum(power) / cells) + 1e-06
        keep = power / (power + lam)
        re, im = transform(False, f_re * keep, f_im * keep)
        re, im = re * (1.0 / cells), im * (1.0 / cells)
    out_ref[0] = re
    out_ref[1] = im


def mwni(sums, counts, tables):
    vmem = pl.BlockSpec(memory_space=pltpu.VMEM)
    return pl.pallas_call(
        mwni_kernel,
        out_shape=jax.ShapeDtypeStruct((2, 256, 256), F32),
        in_specs=[vmem] * 3,
        out_specs=vmem,
        compiler_params=pltpu.CompilerParams(vmem_limit_bytes=56 * 1024 * 1024),
        name="mwni",
    )(sums, counts, tables)


def local(zn, table, tables, traces, bin_ids, valid, tile_owner):
    tiles = tile_owner.shape[0]
    sums, counts = observe(zn, traces, table, bin_ids.reshape(tiles, TILE), valid.reshape(tiles, TILE), tile_owner)
    state = mwni(sums, counts.reshape(-1, TILE), tables)
    return state.reshape(1, 2, -1)


def solution(mesh):
    zn = mesh.shape["bins"] // YN
    table = dft_table(zn, 250)
    tables = grid_tables()
    in_specs = (P("freq", "bins"), P("bins"), P("bins"), P("bins", None))
    out_specs = P(("bins", "freq"), None, None)

    def run(traces, bin_ids, valid, tile_owner):
        return jax.shard_map(
            functools.partial(local, zn, jnp.asarray(table), jnp.asarray(tables)),
            mesh=mesh, in_specs=in_specs, out_specs=out_specs, check_vma=False,
        )(traces, bin_ids, valid, tile_owner)

    return run
```

```python
import functools
import math

import jax
import jax.numpy as jnp
import numpy as np
from jax import lax
from jax.experimental import pallas as pl
from jax.experimental.pallas import tpu as pltpu
from jax.sharding import PartitionSpec as P

MESH = pl.DeviceIdType.MESH
ITERS = 2
TILE = 128
LB = 1024
YN = 4
XN = 4
CN = 2
NQ = 8
BF_STEPS = 6
NJ = 4
UNROLL = 8
F32 = jnp.float32
BF16 = jnp.bfloat16


def dft_table(zn, samples):
    groups = XN * CN
    total = samples * groups
    x, y, c, z = np.meshgrid(np.arange(XN), np.arange(YN), np.arange(CN), np.arange(zn), indexing="ij")
    freq = (((z * YN + y) * XN + x) * CN + c).reshape(-1)
    phase = ((freq[:, None] + 1) * np.arange(total)[None, :]) % total
    angle = phase.astype(np.float32) * np.float32(2.0 * math.pi / total)
    norm = np.float32(1.0 / math.sqrt(total))
    table = np.stack([np.cos(angle) * norm, -np.sin(angle) * norm], axis=0).astype(BF16)
    rows = table.reshape(2 * freq.size, groups, samples)
    return np.ascontiguousarray(rows.transpose(1, 0, 2))


HIGH = LB // TILE


def observe_kernel(zn, x_hbm, tab_hbm, ids_ref, valid_ref, owner_ref, out_ref, tot_ref,
                   xm, tab, far_out, far_l, far_r, near_r_out, near_l_out, near_l, near_r, fin, early,
                   plane0, plane1, acc0, acc1, cnt, pay, labs, slots, rb, sb, rf, sf, cz,
                   tab_sem, loc_sem, core_send, core_recv, far_send, far_recv, near_send, near_recv,
                   y_send, y_recv, own_sem, lab_send, lab_recv, lab_own, slot_sem,
                   b_send, b_recv, f_send, f_recv, cz_own, cz_send, cz_recv, g_send, g_recv):
    bins = lax.axis_index("bins")
    freq = lax.axis_index("freq")
    z, y = bins // YN, bins % YN
    x, c = freq // CN, freq % CN
    nq, chunk = xm.shape[1], xm.shape[3]
    per_chunk = chunk // TILE
    half = nq * chunk
    blk = tab.shape[1] // XN // 2
    part = blk // (YN * CN)
    tiles = ids_ref.shape[0]
    owners = zn * YN
    hops = zn // 2
    rows = acc0.shape[1]
    nj = NJ
    per = rows // nj
    crow = cz.shape[1]
    place = (y * XN + x) * CN + c
    spectra, accs = (plane0, plane1), (acc0, acc1)

    right = (bins, lax.rem(x + 1, XN) * CN + c)
    left = (bins, lax.rem(x + XN - 1, XN) * CN + c)
    other = (bins, x * CN + (1 - c))

    def plane(dy, dc):
        return (z * YN + lax.rem(y + dy, YN), x * CN + lax.rem(c + dc, CN))

    def along_z(dz):
        return (lax.rem(z + dz, zn) * YN + y, freq)

    peers = [(dy, dc) for dy in range(YN) for dc in range(CN) if (dy, dc) != (0, 0)]
    x_peer = [(bins, lax.rem(x + dx, XN) * CN + c) for dx in range(1, XN)]
    y_peer = [plane(dy, 0) for dy in range(1, YN)]

    def remote(src, dst, send, recv, device):
        return pltpu.make_async_remote_copy(
            src_ref=src, dst_ref=dst, send_sem=send, recv_sem=recv, device_id=device, device_id_type=MESH)

    tab_copy = pltpu.make_async_copy(tab_hbm.at[pl.ds(x * CN, CN)], tab, tab_sem)
    tab_copy.start()

    def piece_of(side, q):
        return x_hbm.at[:, pl.ds(pl.multiple_of(side * half + q * chunk, chunk), chunk)]

    def local_copy(q):
        return pltpu.make_async_copy(piece_of(c, q), xm.at[c, q], loc_sem.at[q])

    def core_copy(q):
        return remote(piece_of(1 - c, q), xm.at[c, q], core_send.at[q], core_recv.at[q], other)

    def core_arrival(q):
        return remote(piece_of(c, q), xm.at[1 - c, q], core_send.at[q], core_recv.at[q], other)

    @pl.loop(0, nq)
    def _(q):
        local_copy(q).start()

    barrier = pltpu.get_barrier_semaphore()
    for device in [left, right] + [plane(dy, dc) for dy, dc in peers]:
        pl.semaphore_signal(barrier, inc=1, device_id=device, device_id_type=MESH)
    pl.semaphore_signal(barrier, inc=1, device_id=x_peer[1], device_id_type=MESH)

    for side in (0, 1):
        pl.semaphore_signal(barrier, inc=1, device_id=along_z(1 + side * (zn - 2)), device_id_type=MESH)

    pay[:tiles] = jnp.where(valid_ref[...] > 0, ids_ref[...], LB)
    tile_no = lax.broadcasted_iota(jnp.int32, (owners, tiles), 1)
    named = owner_ref[...] == lax.broadcasted_iota(jnp.int32, (owners, tiles), 0)
    none = tiles + owners
    first = jnp.min(jnp.where(named, tile_no, none), axis=1, keepdims=True)
    second = jnp.max(jnp.where(named, tile_no, -1), axis=1, keepdims=True)
    second = jnp.where(second > first, second, none)
    lane = lax.broadcasted_iota(jnp.int32, (owners, TILE), 1)
    pay[tiles:none] = jnp.where(lane == 0, first, jnp.where(lane == 1, second, LB))
    pay[none:] = jnp.full((8, TILE), LB, jnp.int32)

    pl.semaphore_wait(barrier, 5 + len(peers))

    @pl.loop(0, nq)
    def _(q):
        core_copy(q).start()

    def lab_copy(dy):
        return remote(pay, labs.at[y], lab_send.at[dy - 1], lab_recv.at[dy - 1], plane(dy, 0))

    lab_local = pltpu.make_async_copy(pay, labs.at[y], lab_own)
    lab_local.start()
    for dy in range(1, YN):
        lab_copy(dy).start()

    def product(h, dest, q):
        block = pl.ds(pl.multiple_of(h * (blk * XN) + dest * blk, blk), blk)
        return (jnp.dot(tab[0, block, :], xm[0, q], preferred_element_type=F32)
                + jnp.dot(tab[1, block, :], xm[1, q], preferred_element_type=F32))

    def far_copy(hq, side):
        target, land = ((right, far_l), (left, far_r))[side]
        return remote(far_out.at[hq, pl.ds(side * (blk // 2), blk // 2)], land.at[hq],
                      far_send.at[side, hq], far_recv.at[side, hq], target)

    def near_copy(hq, side):
        target, source, land = ((right, near_r_out, near_l), (left, near_l_out, near_r))[side]
        return remote(source.at[hq], land.at[hq], near_send.at[side, hq], near_recv.at[side, hq], target)

    def y_copy(h, q, i):
        dy, dc = peers[i]
        block = pl.ds(pl.multiple_of((lax.rem(y + dy, YN) * CN + lax.rem(c + dc, CN)) * part, part), part)
        return remote(fin.at[h * nq + q, :, block], spectra[h].at[(y * CN + c) * nq + q],
                      y_send.at[h, i, q], y_recv.at[h, i, q], plane(dy, dc))

    def own_copy(h, q):
        block = pl.ds(pl.multiple_of((y * CN + c) * part, part), part)
        return pltpu.make_async_copy(
            fin.at[h * nq + q, :, block], spectra[h].at[(y * CN + c) * nq + q], own_sem.at[h, q])

    def far_step(h, q):
        hq = h * nq + q
        far_out[hq] = product(h, lax.rem(x + 2, XN), q).astype(BF16)
        far_copy(hq, 0).start()
        far_copy(hq, 1).start()

    def near_step(h, q):
        hq = h * nq + q
        to_right = early[0, q] if h else product(h, lax.rem(x + 1, XN), q)
        to_left = early[1, q] if h else product(h, lax.rem(x + XN - 1, XN), q)
        mid = blk // 2
        far_copy(hq, 0).wait_recv()
        near_r_out[hq, :mid] = (to_right[:mid] + far_l[hq].astype(F32)).astype(BF16)
        near_r_out[hq, mid:] = to_right[mid:].astype(BF16)
        near_copy(hq, 0).start()
        far_copy(hq, 1).wait_recv()
        near_l_out[hq, :mid] = to_left[:mid].astype(BF16)
        near_l_out[hq, mid:] = (to_left[mid:] + far_r[hq].astype(F32)).astype(BF16)
        near_copy(hq, 1).start()

    def final_step(h, q):
        hq = h * nq + q
        mine = early[2, q] if h else product(h, x, q)
        near_copy(hq, 0).wait_recv()
        near_copy(hq, 1).wait_recv()
        full = (mine + (near_l[hq].astype(F32) + near_r[hq].astype(F32))).astype(BF16)
        for r in range(per_chunk):
            fin[hq, r] = full[:, r * TILE:(r + 1) * TILE]
        for i in range(len(peers)):
            y_copy(h, q, i).start()
        own_copy(h, q).start()

    low_iota = [(lax.broadcasted_iota(jnp.int32, (16, TILE), 0) + 16 * i).astype(F32).astype(BF16)
                for i in range(TILE // 16)]
    one, zero = jnp.ones((16, TILE), BF16), jnp.zeros((16, TILE), BF16)

    def bin_owner(h, o):
        lefts, rights = [], []
        for yy in range(YN):
            for rank in range(2):
                t = jnp.clip(slots[yy, o, rank], 0, none)
                label = labs[yy, pl.ds(t, 1), :]
                tv = jnp.minimum(t, tiles - 1)
                vals = spectra[h][yy * (tiles // per_chunk) + tv // per_chunk, tv % per_chunk]
                low = jnp.broadcast_to((label & (TILE - 1)).astype(F32), (16, TILE)).astype(BF16)
                high = jnp.broadcast_to((label // TILE).astype(F32), (16, TILE)).astype(BF16)
                pieces = [jnp.where(high == jnp.asarray(k, BF16), vals, zero) for k in range(HIGH)]
                if h == 0:
                    pieces.append(jnp.where(high == low_iota[0], one, zero))
                lefts.append(jnp.concatenate(pieces, axis=0))
                rights.append(jnp.concatenate([jnp.where(low == it, one, zero) for it in low_iota], axis=0))
        sums = lax.dot_general(jnp.concatenate(lefts, axis=1), jnp.concatenate(rights, axis=1),
                               (((1,), (1,)), ((), ())), preferred_element_type=F32)
        where = pl.ds(pl.multiple_of(o * HIGH, HIGH), HIGH)
        accs[h][:, where, :] = jnp.swapaxes(sums[: HIGH * part].reshape(HIGH, part, TILE), 0, 1)
        if h == 0:
            cnt[where, :] = sums[HIGH * part: HIGH * part + HIGH]

    def bin_range(h, j):
        count = per // HIGH

        @pl.loop(0, count, step=UNROLL)
        def _(k):
            for u in range(UNROLL):
                bin_owner(h, j * count + k + u)

    def next_z(side):
        return along_z(1 + side * (zn - 2))

    def b_copy(h, side, s, j):
        return remote(sb.at[h, side, s, j], rb.at[h, side, s, j],
                      b_send.at[h, side, s, j], b_recv.at[h, side, s, j], next_z(side))

    def f_copy(h, side, s, j):
        k = s - BF_STEPS
        return remote(sf.at[h, side, k, j], rf.at[h, side, k, j],
                      f_send.at[h, side, k, j], f_recv.at[h, side, k, j], next_z(side))

    def z_send(h, side, s, j, value):
        if s < BF_STEPS:
            sb[h, side, s, j] = value.astype(BF16)
            b_copy(h, side, s, j).start()
        else:
            sf[h, side, s - BF_STEPS, j] = value
            f_copy(h, side, s, j).start()

    def z_take(h, side, s, j):
        if s < BF_STEPS:
            b_copy(h, side, s, j).wait_recv()
            return rb[h, side, s, j].astype(F32)
        f_copy(h, side, s, j).wait_recv()
        return rf[h, side, s - BF_STEPS, j]

    def own_bins(h, side, s, j):
        dest = lax.rem(z + hops - s + side * (2 * s), zn)
        return accs[h][dest, pl.ds(pl.multiple_of(j * per, per), per), :]

    def z_second(h, j):
        side = j // (nj // 2)
        z_send(h, side, 1, j, own_bins(h, side, 1, j) + z_take(h, side, 0, j))
        z_send(h, 1 - side, 1, j, own_bins(h, 1 - side, 1, j))

    def z_first_steps(h):
        @pl.loop(0, nj)
        def _(j):
            bin_range(h, j)
            side = j // (nj // 2)
            z_send(h, side, 0, j, own_bins(h, side, 0, j))

            @pl.when(j > 0)
            def _():
                z_second(h, j - 1)

        z_second(h, nj - 1)

    def z_step(h, s, beside=None):
        @pl.loop(0, nj)
        def _(j):
            for side in (0, 1):
                z_send(h, side, s, j, own_bins(h, side, s, j) + z_take(h, side, s - 1, j))
            if beside is not None:
                beside(j)

    def z_final(h):
        @pl.loop(0, nj)
        def _(j):
            value = z_take(h, 0, hops - 1, j) + z_take(h, 1, hops - 1, j)
            out_ref[h, pl.ds(pl.multiple_of(j * per, per), per), :] = value + own_bins(h, 0, hops, j)

    mine_rows = pl.ds(pl.multiple_of(place * crow, crow), crow)

    def cz_copy(hop, side):
        slot = lax.rem(z + zn + (2 * side - 1) * (hop - 1), zn)
        return remote(cz.at[slot], cz.at[slot], cz_send.at[side, hop - 1], cz_recv.at[side, hop - 1], next_z(side))

    def counts_onward(hop):
        if hop > 1:
            for side in (0, 1):
                cz_copy(hop - 1, side).wait_recv()
        for side in ((0, 1) if hop < hops else (0,)):
            cz_copy(hop, side).start()

    cnt_own = pltpu.make_async_copy(cnt.at[mine_rows], cz.at[z], cz_own)

    def gather(i, size, device):
        part_of = pl.ds(place // size * size, size)
        return remote(tot_ref.at[part_of], tot_ref.at[part_of], g_send.at[i], g_recv.at[i], device)

    stages = [
        [(0, 1, other)],
        [(1 + i, CN, device) for i, device in enumerate(x_peer)],
        [(XN + i, CN * XN, device) for i, device in enumerate(y_peer)],
    ]

    tab_copy.wait()

    @pl.loop(0, nq)
    def _(q):
        local_copy(q).wait()
        core_arrival(q).wait_recv()
        far_step(0, q)

    for dy in range(1, YN):
        lab_copy(dy).wait()
    lab_local.wait()
    slot_copy = pltpu.make_async_copy(labs.at[:, pl.ds(tiles, owners)], slots, slot_sem)
    slot_copy.start()

    @pl.loop(0, nq)
    def _(q):
        near_step(0, q)

    @pl.loop(0, nq)
    def _(q):
        final_step(0, q)
        far_step(1, q)
        early[0, q] = product(1, lax.rem(x + 1, XN), q)
        early[1, q] = product(1, lax.rem(x + XN - 1, XN), q)
        early[2, q] = product(1, x, q)

    slot_copy.wait()

    def plane_arrived(h):
        @pl.loop(0, nq)
        def _(q):
            for i in range(len(peers)):
                y_copy(h, q, i).wait_recv()
            own_copy(h, q).wait()

    plane_arrived(0)
    z_first_steps(0)
    cnt_own.start()
    cnt_own.wait()
    counts_onward(1)

    quarter = nq // (2 * nj)

    def near_beside(first):
        def work(j):
            for i in range(quarter):
                near_step(1, first + j * quarter + i)
        return work

    def final_beside(first):
        def work(j):
            for i in range(quarter):
                final_step(1, first + j * quarter + i)
        return work

    z_step(0, 2, near_beside(0))
    counts_onward(2)
    z_step(0, 3, near_beside(nq // 2))
    counts_onward(3)
    z_step(0, 4)
    counts_onward(4)
    z_step(0, 5)
    counts_onward(5)
    z_step(0, 6, final_beside(0))
    counts_onward(6)
    z_step(0, 7)
    counts_onward(7)

    @pl.loop(nq // 2, nq)
    def _(q):
        final_step(1, q)

    plane_arrived(1)
    z_first_steps(1)
    counts_onward(8)
    z_final(0)
    z_step(1, 2)
    cz_copy(8, 0).wait_recv()
    tot_ref[pl.ds(place, 1)] = jnp.sum(cz[...], axis=0)[None]
    for args in stages[0]:
        gather(*args).start()
    z_step(1, 3)
    for args in stages[0]:
        gather(*args).wait()
    for args in stages[1]:
        gather(*args).start()
    z_step(1, 4)
    for args in stages[1]:
        gather(*args).wait()
    for args in stages[2]:
        gather(*args).start()
    for s in range(5, hops):
        z_step(1, s)
    z_final(1)
    for args in stages[2]:
        gather(*args).wait()

    @pl.loop(0, nq)
    def _(q):
        core_copy(q).wait_send()
        for h in (0, 1):
            for side in (0, 1):
                far_copy(h * nq + q, side).wait_send()
                near_copy(h * nq + q, side).wait_send()
            for i in range(len(peers)):
                y_copy(h, q, i).wait_send()

    for hop in range(1, hops + 1):
        for side in ((0, 1) if hop < hops else (0,)):
            cz_copy(hop, side).wait_send()

    @pl.loop(0, nj)
    def _(j):
        for h in (0, 1):
            b_copy(h, j // (nj // 2), 0, j).wait_send()

            @pl.loop(1, BF_STEPS)
            def _(s):
                for side in (0, 1):
                    b_copy(h, side, s, j).wait_send()

            @pl.loop(BF_STEPS, hops)
            def _(s):
                for side in (0, 1):
                    f_copy(h, side, s, j).wait_send()


def observe(zn, traces, table, ids, valid, owner):
    samples, width = traces.shape
    _, table_rows, _ = table.shape
    half = width // CN
    nq = NQ
    chunk = half // nq
    blk = table_rows // XN // 2
    part = blk // (YN * CN)
    tiles = ids.shape[0]
    hops = zn // 2
    fs = hops - BF_STEPS
    owners = zn * YN
    rows = owners * HIGH
    per = rows // NJ
    places = YN * XN * CN
    crow = rows // places
    npeer = YN * CN - 1
    dma = pltpu.SemaphoreType.DMA
    any_spec = pl.BlockSpec(memory_space=pl.ANY)
    vmem = pl.BlockSpec(memory_space=pltpu.VMEM)
    plane_buf = pltpu.VMEM((YN * CN * nq, chunk // TILE, part, TILE), BF16)
    return pl.pallas_call(
        functools.partial(observe_kernel, zn),
        out_shape=(
            jax.ShapeDtypeStruct((2, rows, TILE), F32),
            jax.ShapeDtypeStruct((places, crow, TILE), F32),
        ),
        in_specs=[any_spec, any_spec, vmem, vmem, vmem],
        out_specs=(vmem, vmem),
        scratch_shapes=[
            pltpu.VMEM((CN, nq, samples, chunk), BF16),
            pltpu.VMEM((CN, table_rows, samples), BF16),
            pltpu.VMEM((2 * nq, blk, chunk), BF16),
            pltpu.VMEM((2 * nq, blk // 2, chunk), BF16),
            pltpu.VMEM((2 * nq, blk // 2, chunk), BF16),
            pltpu.VMEM((2 * nq, blk, chunk), BF16),
            pltpu.VMEM((2 * nq, blk, chunk), BF16),
            pltpu.VMEM((2 * nq, blk, chunk), BF16),
            pltpu.VMEM((2 * nq, blk, chunk), BF16),
            pltpu.VMEM((2 * nq, chunk // TILE, blk, TILE), BF16),
            pltpu.VMEM((XN - 1, nq, blk, chunk), F32),
            plane_buf, plane_buf,
            pltpu.VMEM((part, rows, TILE), F32),
            pltpu.VMEM((part, rows, TILE), F32),
            pltpu.VMEM((rows, TILE), F32),
            pltpu.VMEM((tiles + owners + 8, TILE), jnp.int32),
            pltpu.VMEM((YN, tiles + owners + 8, TILE), jnp.int32),
            pltpu.SMEM((YN, owners, TILE), jnp.int32),
            pltpu.VMEM((2, 2, BF_STEPS, NJ, per, TILE), BF16),
            pltpu.VMEM((2, 2, BF_STEPS, NJ, per, TILE), BF16),
            pltpu.VMEM((2, 2, fs, NJ, per, TILE), F32),
            pltpu.VMEM((2, 2, fs, NJ, per, TILE), F32),
            pltpu.VMEM((zn, crow, TILE), F32),
            dma, dma((nq,)), dma((nq,)), dma((nq,)),
            dma((2, 2 * nq)), dma((2, 2 * nq)), dma((2, 2 * nq)), dma((2, 2 * nq)),
            dma((2, npeer, nq)), dma((2, npeer, nq)), dma((2, nq)),
            dma((YN - 1,)), dma((YN - 1,)), dma, dma,
            dma((2, 2, BF_STEPS, NJ)), dma((2, 2, BF_STEPS, NJ)), dma((2, 2, fs, NJ)), dma((2, 2, fs, NJ)),
            dma, dma((2, hops)), dma((2, hops)), dma((7,)), dma((7,)),
        ],
        compiler_params=pltpu.CompilerParams(
            collective_id=0, has_side_effects=True, vmem_limit_bytes=60 * 1024 * 1024),
        cost_estimate=pl.CostEstimate(flops=2 * table_rows * samples * width, bytes_accessed=12 << 20, transcendentals=0),
        name="observe",
    )(traces, table, ids, valid, owner)


def grid_tables():
    index = np.arange(256)
    a, b = index // 16, index % 16
    phase = (a[:, None] * a[None, :] + b[:, None] * b[None, :]) % 16
    angle = 2.0 * np.pi * phase / 16.0
    both = np.concatenate([np.cos(angle), np.sin(angle)], axis=1).astype(np.float32)
    hi = both.astype(BF16)
    return np.stack([hi, (both - hi.astype(np.float32)).astype(BF16)])


def split(value):
    hi = value.astype(BF16)
    return hi, (value - hi.astype(F32)).astype(BF16)


def mwni_kernel(sum_ref, cnt_ref, tab_ref, out_ref):
    n = 256
    cells = n * n

    def grid(ref):
        return jnp.concatenate([ref[pl.ds(0, n, stride=2), :], ref[pl.ds(1, n, stride=2), :]], axis=1)

    t_hi, t_lo = tab_ref[0], tab_ref[1]
    r_hi = jnp.concatenate([t_hi[:, :n], t_hi[:, n:]], axis=0)
    r_lo = jnp.concatenate([t_lo[:, :n], t_lo[:, n:]], axis=0)
    dot = functools.partial(jnp.dot, preferred_element_type=F32)

    def transform(sign, re, im):
        def left(a, b):
            low = [b, -a] if sign > 0 else [-b, a]
            return jnp.concatenate([jnp.concatenate([a, b], axis=1), jnp.concatenate(low, axis=1)], axis=0)

        def right(a, b):
            first, second = ([a, b], [b, -a]) if sign > 0 else ([a, -b], [b, a])
            return jnp.concatenate([jnp.concatenate(first, axis=1), jnp.concatenate(second, axis=1)], axis=0)

        (re_hi, re_lo), (im_hi, im_lo) = split(re), split(im)
        hi, lo = left(re_hi, im_hi), left(re_lo, im_lo)
        mid = dot(t_hi, hi) + (dot(t_hi, lo) + dot(t_lo, hi))
        (re_hi, re_lo), (im_hi, im_lo) = split(mid[:, :n]), split(mid[:, n:])
        hi, lo = right(re_hi, im_hi), right(re_lo, im_lo)
        out = dot(hi, r_hi) + (dot(lo, r_hi) + dot(hi, r_lo))
        return out[:n], out[n:]

    count = grid(cnt_ref)
    cover = jnp.minimum(count, 1.0)
    scale = 1.0 / jnp.maximum(count, 1.0)
    obs_re = grid(sum_ref.at[0]) * scale
    obs_im = grid(sum_ref.at[1]) * scale
    re, im = obs_re, obs_im
    for step in range(ITERS):
        u_re = cover * obs_re + (1.0 - cover) * re
        u_im = cover * obs_im + (1.0 - cover) * im
        f_re, f_im = transform(1, u_re, u_im)
        power = f_re * f_re + f_im * f_im
        lam = 0.5 * (jnp.sum(power) / cells) + 1e-06
        keep = power / (power + lam)
        re, im = transform(-1, f_re * keep, f_im * keep)
        re, im = re * (1.0 / cells), im * (1.0 / cells)
    for part, value in enumerate((re, im)):
        for side in range(2):
            out_ref[pl.ds(2 * side + part, n, stride=4), :] = value[:, side * TILE:(side + 1) * TILE]


def mwni(sums, counts, tables):
    vmem = pl.BlockSpec(memory_space=pltpu.VMEM)
    return pl.pallas_call(
        mwni_kernel,
        out_shape=jax.ShapeDtypeStruct((1024, TILE), F32),
        in_specs=[vmem] * 3,
        out_specs=vmem,
        compiler_params=pltpu.CompilerParams(vmem_limit_bytes=56 * 1024 * 1024),
        name="mwni",
    )(sums, counts, tables)


def local(zn, table, tables, traces, bin_ids, valid, tile_owner):
    tiles = tile_owner.shape[0]
    sums, counts = observe(zn, traces, table, bin_ids.reshape(tiles, TILE), valid.reshape(tiles, TILE),
                           tile_owner.reshape(1, tiles))
    state = mwni(sums, counts.reshape(-1, TILE), tables)
    return state.reshape(-1, 2, TILE).transpose(1, 0, 2).reshape(1, 2, -1)


def solution(mesh):
    zn = mesh.shape["bins"] // YN
    table = dft_table(zn, 250)
    tables = grid_tables()
    in_specs = (P("freq", "bins"), P("bins"), P("bins"), P("bins", None))
    out_specs = P(("bins", "freq"), None, None)

    def run(traces, bin_ids, valid, tile_owner):
        return jax.shard_map(
            functools.partial(local, zn, jnp.asarray(table), jnp.asarray(tables)),
            mesh=mesh, in_specs=in_specs, out_specs=out_specs, check_vma=False,
        )(traces, bin_ids, valid, tile_owner)

    return run
```

```python
import functools
import math

import jax
import jax.numpy as jnp
import numpy as np
from jax import lax
from jax.experimental import pallas as pl
from jax.experimental.pallas import tpu as pltpu
from jax.sharding import PartitionSpec as P

MESH = pl.DeviceIdType.MESH
ITERS = 2
TILE = 128
LB = 1024
YN = 4
XN = 4
CN = 2
NQ = 8
BF_STEPS = 7
NJ = 4
UNROLL = 8
F32 = jnp.float32
BF16 = jnp.bfloat16


def dft_table(zn, samples):
    groups = XN * CN
    total = samples * groups
    x, y, c, z = np.meshgrid(np.arange(XN), np.arange(YN), np.arange(CN), np.arange(zn), indexing="ij")
    freq = (((z * YN + y) * XN + x) * CN + c).reshape(-1)
    phase = ((freq[:, None] + 1) * np.arange(total)[None, :]) % total
    angle = phase.astype(np.float32) * np.float32(2.0 * math.pi / total)
    norm = np.float32(1.0 / math.sqrt(total))
    table = np.stack([np.cos(angle) * norm, -np.sin(angle) * norm], axis=0).astype(BF16)
    rows = table.reshape(2 * freq.size, groups, samples)
    return np.ascontiguousarray(rows.transpose(1, 0, 2))


HIGH = LB // TILE


def observe_kernel(zn, x_hbm, tab_hbm, ids_ref, valid_ref, owner_ref, out_ref, tot_ref,
                   xm, tab, far_out, far_l, far_r, near_r_out, near_l_out, near_l, near_r, fin, early,
                   plane0, plane1, acc0, acc1, cnt, pay, labs, slots, rb, sb, rf, sf, cz,
                   tab_sem, loc_sem, core_send, core_recv, far_send, far_recv, near_send, near_recv,
                   y_send, y_recv, own_sem, lab_send, lab_recv, lab_own, slot_sem,
                   b_send, b_recv, f_send, f_recv, cz_own, cz_send, cz_recv, g_send, g_recv):
    bins = lax.axis_index("bins")
    freq = lax.axis_index("freq")
    z, y = bins // YN, bins % YN
    x, c = freq // CN, freq % CN
    nq, chunk = xm.shape[1], xm.shape[3]
    per_chunk = chunk // TILE
    half = nq * chunk
    blk = tab.shape[1] // XN // 2
    part = blk // (YN * CN)
    tiles = ids_ref.shape[0]
    owners = zn * YN
    hops = zn // 2
    rows = acc0.shape[1]
    nj = NJ
    per = rows // nj
    crow = cz.shape[1]
    place = (y * XN + x) * CN + c
    spectra, accs = (plane0, plane1), (acc0, acc1)

    right = (bins, lax.rem(x + 1, XN) * CN + c)
    left = (bins, lax.rem(x + XN - 1, XN) * CN + c)
    other = (bins, x * CN + (1 - c))

    def plane(dy, dc):
        return (z * YN + lax.rem(y + dy, YN), x * CN + lax.rem(c + dc, CN))

    def along_z(dz):
        return (lax.rem(z + dz, zn) * YN + y, freq)

    peers = [(dy, dc) for dy in range(YN) for dc in range(CN) if (dy, dc) != (0, 0)]
    x_peer = [(bins, lax.rem(x + dx, XN) * CN + c) for dx in range(1, XN)]
    y_peer = [plane(dy, 0) for dy in range(1, YN)]

    def remote(src, dst, send, recv, device):
        return pltpu.make_async_remote_copy(
            src_ref=src, dst_ref=dst, send_sem=send, recv_sem=recv, device_id=device, device_id_type=MESH)

    tab_copy = pltpu.make_async_copy(tab_hbm.at[pl.ds(x * CN, CN)], tab, tab_sem)
    tab_copy.start()

    def piece_of(side, q):
        return x_hbm.at[:, pl.ds(pl.multiple_of(side * half + q * chunk, chunk), chunk)]

    def local_copy(q):
        return pltpu.make_async_copy(piece_of(c, q), xm.at[c, q], loc_sem.at[q])

    def core_copy(q):
        return remote(piece_of(1 - c, q), xm.at[c, q], core_send.at[q], core_recv.at[q], other)

    def core_arrival(q):
        return remote(piece_of(c, q), xm.at[1 - c, q], core_send.at[q], core_recv.at[q], other)

    @pl.loop(0, nq)
    def _(q):
        local_copy(q).start()

    barrier = pltpu.get_barrier_semaphore()
    for device in [left, right] + [plane(dy, dc) for dy, dc in peers]:
        pl.semaphore_signal(barrier, inc=1, device_id=device, device_id_type=MESH)
    pl.semaphore_signal(barrier, inc=1, device_id=x_peer[1], device_id_type=MESH)

    for side in (0, 1):
        pl.semaphore_signal(barrier, inc=1, device_id=along_z(1 + side * (zn - 2)), device_id_type=MESH)

    pay[:tiles] = jnp.where(valid_ref[...] > 0, ids_ref[...], LB)
    tile_no = lax.broadcasted_iota(jnp.int32, (owners, tiles), 1)
    named = owner_ref[...] == lax.broadcasted_iota(jnp.int32, (owners, tiles), 0)
    none = tiles + owners
    first = jnp.min(jnp.where(named, tile_no, none), axis=1, keepdims=True)
    second = jnp.max(jnp.where(named, tile_no, -1), axis=1, keepdims=True)
    second = jnp.where(second > first, second, none)
    lane = lax.broadcasted_iota(jnp.int32, (owners, TILE), 1)
    pay[tiles:none] = jnp.where(lane == 0, first, jnp.where(lane == 1, second, LB))
    pay[none:] = jnp.full((8, TILE), LB, jnp.int32)

    pl.semaphore_wait(barrier, 5 + len(peers))

    @pl.loop(0, nq)
    def _(q):
        core_copy(q).start()

    def lab_copy(dy):
        return remote(pay, labs.at[y], lab_send.at[dy - 1], lab_recv.at[dy - 1], plane(dy, 0))

    lab_local = pltpu.make_async_copy(pay, labs.at[y], lab_own)
    lab_local.start()
    for dy in range(1, YN):
        lab_copy(dy).start()

    def product(h, dest, q):
        block = pl.ds(pl.multiple_of(h * (blk * XN) + dest * blk, blk), blk)
        return (jnp.dot(tab[0, block, :], xm[0, q], preferred_element_type=F32)
                + jnp.dot(tab[1, block, :], xm[1, q], preferred_element_type=F32))

    def far_copy(hq, side):
        target, land = ((right, far_l), (left, far_r))[side]
        return remote(far_out.at[hq, pl.ds(side * (blk // 2), blk // 2)], land.at[hq],
                      far_send.at[side, hq], far_recv.at[side, hq], target)

    def near_copy(hq, side):
        target, source, land = ((right, near_r_out, near_l), (left, near_l_out, near_r))[side]
        return remote(source.at[hq], land.at[hq], near_send.at[side, hq], near_recv.at[side, hq], target)

    def y_copy(h, q, i):
        dy, dc = peers[i]
        block = pl.ds(pl.multiple_of((lax.rem(y + dy, YN) * CN + lax.rem(c + dc, CN)) * part, part), part)
        return remote(fin.at[h * nq + q, :, block], spectra[h].at[(y * CN + c) * nq + q],
                      y_send.at[h, i, q], y_recv.at[h, i, q], plane(dy, dc))

    def own_copy(h, q):
        block = pl.ds(pl.multiple_of((y * CN + c) * part, part), part)
        return pltpu.make_async_copy(
            fin.at[h * nq + q, :, block], spectra[h].at[(y * CN + c) * nq + q], own_sem.at[h, q])

    def far_step(h, q):
        hq = h * nq + q
        far_out[hq] = product(h, lax.rem(x + 2, XN), q).astype(BF16)
        far_copy(hq, 0).start()
        far_copy(hq, 1).start()

    def near_step(h, q):
        hq = h * nq + q
        to_right = early[0, q] if h else product(h, lax.rem(x + 1, XN), q)
        to_left = early[1, q] if h else product(h, lax.rem(x + XN - 1, XN), q)
        mid = blk // 2
        far_copy(hq, 0).wait_recv()
        near_r_out[hq, :mid] = (to_right[:mid] + far_l[hq].astype(F32)).astype(BF16)
        near_r_out[hq, mid:] = to_right[mid:].astype(BF16)
        near_copy(hq, 0).start()
        far_copy(hq, 1).wait_recv()
        near_l_out[hq, :mid] = to_left[:mid].astype(BF16)
        near_l_out[hq, mid:] = (to_left[mid:] + far_r[hq].astype(F32)).astype(BF16)
        near_copy(hq, 1).start()

    def final_step(h, q):
        hq = h * nq + q
        mine = early[2, q] if h else product(h, x, q)
        near_copy(hq, 0).wait_recv()
        near_copy(hq, 1).wait_recv()
        full = (mine + (near_l[hq].astype(F32) + near_r[hq].astype(F32))).astype(BF16)
        for r in range(per_chunk):
            fin[hq, r] = full[:, r * TILE:(r + 1) * TILE]
        for i in range(len(peers)):
            y_copy(h, q, i).start()
        own_copy(h, q).start()

    low_iota = [(lax.broadcasted_iota(jnp.int32, (16, TILE), 0) + 16 * i).astype(F32).astype(BF16)
                for i in range(TILE // 16)]
    one, zero = jnp.ones((16, TILE), BF16), jnp.zeros((16, TILE), BF16)

    def bin_owner(h, o):
        lefts, rights = [], []
        for yy in range(YN):
            for rank in range(2):
                t = jnp.clip(slots[yy, o, rank], 0, none)
                label = labs[yy, pl.ds(t, 1), :]
                tv = jnp.minimum(t, tiles - 1)
                vals = spectra[h][yy * (tiles // per_chunk) + tv // per_chunk, tv % per_chunk]
                low = jnp.broadcast_to((label & (TILE - 1)).astype(F32), (16, TILE)).astype(BF16)
                high = jnp.broadcast_to((label // TILE).astype(F32), (16, TILE)).astype(BF16)
                pieces = [jnp.where(high == jnp.asarray(k, BF16), vals, zero) for k in range(HIGH)]
                if h == 0:
                    pieces.append(jnp.where(high == low_iota[0], one, zero))
                lefts.append(jnp.concatenate(pieces, axis=0))
                rights.append(jnp.concatenate([jnp.where(low == it, one, zero) for it in low_iota], axis=0))
        sums = lax.dot_general(jnp.concatenate(lefts, axis=1), jnp.concatenate(rights, axis=1),
                               (((1,), (1,)), ((), ())), preferred_element_type=F32)
        where = pl.ds(pl.multiple_of(o * HIGH, HIGH), HIGH)
        accs[h][:, where, :] = jnp.swapaxes(sums[: HIGH * part].reshape(HIGH, part, TILE), 0, 1)
        if h == 0:
            cnt[where, :] = sums[HIGH * part: HIGH * part + HIGH]

    def bin_range(h, j):
        count = per // HIGH

        @pl.loop(0, count, step=UNROLL)
        def _(k):
            for u in range(UNROLL):
                bin_owner(h, j * count + k + u)

    def next_z(side):
        return along_z(1 + side * (zn - 2))

    def b_copy(h, side, s, j):
        return remote(sb.at[h, side, s, j], rb.at[h, side, s, j],
                      b_send.at[h, side, s, j], b_recv.at[h, side, s, j], next_z(side))

    def f_copy(h, side, s, j):
        k = s - BF_STEPS
        return remote(sf.at[h, side, k, j], rf.at[h, side, k, j],
                      f_send.at[h, side, k, j], f_recv.at[h, side, k, j], next_z(side))

    def z_send(h, side, s, j, value):
        if s < BF_STEPS:
            sb[h, side, s, j] = value.astype(BF16)
            b_copy(h, side, s, j).start()
        else:
            sf[h, side, s - BF_STEPS, j] = value
            f_copy(h, side, s, j).start()

    def z_take(h, side, s, j):
        if s < BF_STEPS:
            b_copy(h, side, s, j).wait_recv()
            return rb[h, side, s, j].astype(F32)
        f_copy(h, side, s, j).wait_recv()
        return rf[h, side, s - BF_STEPS, j]

    def own_bins(h, side, s, j):
        dest = lax.rem(z + hops - s + side * (2 * s), zn)
        return accs[h][dest, pl.ds(pl.multiple_of(j * per, per), per), :]

    def z_second(h, j):
        side = j // (nj // 2)
        z_send(h, side, 1, j, own_bins(h, side, 1, j) + z_take(h, side, 0, j))
        z_send(h, 1 - side, 1, j, own_bins(h, 1 - side, 1, j))

    def z_first_steps(h):
        @pl.loop(0, nj)
        def _(j):
            bin_range(h, j)
            side = j // (nj // 2)
            z_send(h, side, 0, j, own_bins(h, side, 0, j))

            @pl.when(j > 0)
            def _():
                z_second(h, j - 1)

        z_second(h, nj - 1)

    def z_step(h, s, beside=None):
        @pl.loop(0, nj)
        def _(j):
            for side in (0, 1):
                z_send(h, side, s, j, own_bins(h, side, s, j) + z_take(h, side, s - 1, j))
            if beside is not None:
                beside(j)

    def z_final(h):
        @pl.loop(0, nj)
        def _(j):
            value = z_take(h, 0, hops - 1, j) + z_take(h, 1, hops - 1, j)
            out_ref[h, pl.ds(pl.multiple_of(j * per, per), per), :] = value + own_bins(h, 0, hops, j)

    mine_rows = pl.ds(pl.multiple_of(place * crow, crow), crow)

    def cz_copy(hop, side):
        slot = lax.rem(z + zn + (2 * side - 1) * (hop - 1), zn)
        return remote(cz.at[slot], cz.at[slot], cz_send.at[side, hop - 1], cz_recv.at[side, hop - 1], next_z(side))

    def counts_onward(hop):
        if hop > 1:
            for side in (0, 1):
                cz_copy(hop - 1, side).wait_recv()
        for side in ((0, 1) if hop < hops else (0,)):
            cz_copy(hop, side).start()

    cnt_own = pltpu.make_async_copy(cnt.at[mine_rows], cz.at[z], cz_own)

    def gather(i, size, device):
        part_of = pl.ds(place // size * size, size)
        return remote(tot_ref.at[part_of], tot_ref.at[part_of], g_send.at[i], g_recv.at[i], device)

    stages = [
        [(0, 1, other)],
        [(1 + i, CN, device) for i, device in enumerate(x_peer)],
        [(XN + i, CN * XN, device) for i, device in enumerate(y_peer)],
    ]

    tab_copy.wait()

    @pl.loop(0, nq)
    def _(q):
        local_copy(q).wait()
        core_arrival(q).wait_recv()
        far_step(0, q)

    for dy in range(1, YN):
        lab_copy(dy).wait()
    lab_local.wait()
    slot_copy = pltpu.make_async_copy(labs.at[:, pl.ds(tiles, owners)], slots, slot_sem)
    slot_copy.start()

    @pl.loop(0, nq)
    def _(q):
        near_step(0, q)

    def chunk_arrived(h, q):
        for i in range(len(peers)):
            y_copy(h, q, i).wait_recv()
        own_copy(h, q).wait()

    def plane_arrived(h, first, last):
        @pl.loop(first, last)
        def _(q):
            chunk_arrived(h, q)

    def x_sent(h, q):
        for side in (0, 1):
            far_copy(h * nq + q, side).wait_send()
            near_copy(h * nq + q, side).wait_send()
        for i in range(len(peers)):
            y_copy(h, q, i).wait_send()

    def z_sent(h, j, first, last):
        @pl.loop(first, min(last, BF_STEPS))
        def _(s):
            for side in (0, 1):
                b_copy(h, side, s, j).wait_send()

        if last > BF_STEPS:
            @pl.loop(BF_STEPS, last)
            def _(s):
                for side in (0, 1):
                    f_copy(h, side, s, j).wait_send()

    @pl.loop(0, nq)
    def _(q):
        final_step(0, q)
        far_step(1, q)
        early[0, q] = product(1, lax.rem(x + 1, XN), q)
        early[1, q] = product(1, lax.rem(x + XN - 1, XN), q)
        early[2, q] = product(1, x, q)

        @pl.when(q >= 2)
        def _():
            chunk_arrived(0, q - 2)

    slot_copy.wait()

    plane_arrived(0, nq - 2, nq)
    z_first_steps(0)
    cnt_own.start()
    cnt_own.wait()
    counts_onward(1)

    quarter = nq // (2 * nj)

    def near_beside(first):
        def work(j):
            for i in range(quarter):
                near_step(1, first + j * quarter + i)
        return work

    def final_beside(first):
        def work(j):
            for i in range(quarter):
                final_step(1, first + j * quarter + i)
        return work

    z_step(0, 2, near_beside(0))
    counts_onward(2)
    z_step(0, 3, near_beside(nq // 2))
    counts_onward(3)
    z_step(0, 4)
    counts_onward(4)
    z_step(0, 5)
    counts_onward(5)
    z_step(0, 6, final_beside(0))
    counts_onward(6)
    z_step(0, 7)
    counts_onward(7)

    @pl.loop(0, nq // 2)
    def _(q):
        final_step(1, nq // 2 + q)
        for k in (0, 1):
            core_copy(2 * q + k).wait_send()
            x_sent(0, 2 * q + k)
        chunk_arrived(1, q)

    plane_arrived(1, nq // 2, nq)
    z_first_steps(1)
    counts_onward(8)
    z_final(0)
    z_step(1, 2)
    cz_copy(8, 0).wait_recv()
    tot_ref[pl.ds(place, 1)] = jnp.sum(cz[...], axis=0)[None]
    for args in stages[0]:
        gather(*args).start()
    z_step(1, 3)
    for args in stages[0]:
        gather(*args).wait()
    for args in stages[1]:
        gather(*args).start()
    z_step(1, 4)
    for args in stages[1]:
        gather(*args).wait()
    for args in stages[2]:
        gather(*args).start()
    def x_sent_beside(first):
        def work(j):
            for i in range(quarter):
                x_sent(1, first + j * quarter + i)
        return work

    def z_sent_early(j):
        b_copy(0, j // (nj // 2), 0, j).wait_send()
        b_copy(1, j // (nj // 2), 0, j).wait_send()
        z_sent(0, j, 1, hops)

    z_step(1, 5, x_sent_beside(0))
    z_step(1, 6, x_sent_beside(nq // 2))
    z_step(1, 7, z_sent_early)
    z_final(1)

    for args in stages[2]:
        gather(*args).wait()
    for hop in range(1, hops + 1):
        for side in ((0, 1) if hop < hops else (0,)):
            cz_copy(hop, side).wait_send()

    @pl.loop(0, nj)
    def _(j):
        z_sent(1, j, 1, hops)


def observe(zn, traces, table, ids, valid, owner):
    samples, width = traces.shape
    _, table_rows, _ = table.shape
    half = width // CN
    nq = NQ
    chunk = half // nq
    blk = table_rows // XN // 2
    part = blk // (YN * CN)
    tiles = ids.shape[0]
    hops = zn // 2
    fs = hops - BF_STEPS
    owners = zn * YN
    rows = owners * HIGH
    per = rows // NJ
    places = YN * XN * CN
    crow = rows // places
    npeer = YN * CN - 1
    dma = pltpu.SemaphoreType.DMA
    any_spec = pl.BlockSpec(memory_space=pl.ANY)
    vmem = pl.BlockSpec(memory_space=pltpu.VMEM)
    plane_buf = pltpu.VMEM((YN * CN * nq, chunk // TILE, part, TILE), BF16)
    return pl.pallas_call(
        functools.partial(observe_kernel, zn),
        out_shape=(
            jax.ShapeDtypeStruct((2, rows, TILE), F32),
            jax.ShapeDtypeStruct((places, crow, TILE), F32),
        ),
        in_specs=[any_spec, any_spec, vmem, vmem, vmem],
        out_specs=(vmem, vmem),
        scratch_shapes=[
            pltpu.VMEM((CN, nq, samples, chunk), BF16),
            pltpu.VMEM((CN, table_rows, samples), BF16),
            pltpu.VMEM((2 * nq, blk, chunk), BF16),
            pltpu.VMEM((2 * nq, blk // 2, chunk), BF16),
            pltpu.VMEM((2 * nq, blk // 2, chunk), BF16),
            pltpu.VMEM((2 * nq, blk, chunk), BF16),
            pltpu.VMEM((2 * nq, blk, chunk), BF16),
            pltpu.VMEM((2 * nq, blk, chunk), BF16),
            pltpu.VMEM((2 * nq, blk, chunk), BF16),
            pltpu.VMEM((2 * nq, chunk // TILE, blk, TILE), BF16),
            pltpu.VMEM((XN - 1, nq, blk, chunk), F32),
            plane_buf, plane_buf,
            pltpu.VMEM((part, rows, TILE), F32),
            pltpu.VMEM((part, rows, TILE), F32),
            pltpu.VMEM((rows, TILE), F32),
            pltpu.VMEM((tiles + owners + 8, TILE), jnp.int32),
            pltpu.VMEM((YN, tiles + owners + 8, TILE), jnp.int32),
            pltpu.SMEM((YN, owners, TILE), jnp.int32),
            pltpu.VMEM((2, 2, BF_STEPS, NJ, per, TILE), BF16),
            pltpu.VMEM((2, 2, BF_STEPS, NJ, per, TILE), BF16),
            pltpu.VMEM((2, 2, fs, NJ, per, TILE), F32),
            pltpu.VMEM((2, 2, fs, NJ, per, TILE), F32),
            pltpu.VMEM((zn, crow, TILE), F32),
            dma, dma((nq,)), dma((nq,)), dma((nq,)),
            dma((2, 2 * nq)), dma((2, 2 * nq)), dma((2, 2 * nq)), dma((2, 2 * nq)),
            dma((2, npeer, nq)), dma((2, npeer, nq)), dma((2, nq)),
            dma((YN - 1,)), dma((YN - 1,)), dma, dma,
            dma((2, 2, BF_STEPS, NJ)), dma((2, 2, BF_STEPS, NJ)), dma((2, 2, fs, NJ)), dma((2, 2, fs, NJ)),
            dma, dma((2, hops)), dma((2, hops)), dma((7,)), dma((7,)),
        ],
        compiler_params=pltpu.CompilerParams(
            collective_id=0, has_side_effects=True, vmem_limit_bytes=60 * 1024 * 1024),
        cost_estimate=pl.CostEstimate(flops=2 * table_rows * samples * width, bytes_accessed=12 << 20, transcendentals=0),
        name="observe",
    )(traces, table, ids, valid, owner)


def grid_tables():
    index = np.arange(256)
    a, b = index // 16, index % 16
    phase = (a[:, None] * a[None, :] + b[:, None] * b[None, :]) % 16
    angle = 2.0 * np.pi * phase / 16.0
    both = np.concatenate([np.cos(angle), np.sin(angle)], axis=1).astype(np.float32)
    hi = both.astype(BF16)
    return np.stack([hi, (both - hi.astype(np.float32)).astype(BF16)])


def split(value):
    hi = value.astype(BF16)
    return hi, (value - hi.astype(F32)).astype(BF16)


def mwni_kernel(sum_ref, cnt_ref, tab_ref, out_ref):
    n = 256
    cells = n * n

    def grid(ref):
        return jnp.concatenate([ref[pl.ds(0, n, stride=2), :], ref[pl.ds(1, n, stride=2), :]], axis=1)

    t_hi, t_lo = tab_ref[0], tab_ref[1]
    r_hi = jnp.concatenate([t_hi[:, :n], t_hi[:, n:]], axis=0)
    r_lo = jnp.concatenate([t_lo[:, :n], t_lo[:, n:]], axis=0)
    dot = functools.partial(jnp.dot, preferred_element_type=F32)

    def transform(sign, re, im):
        def left(a, b):
            low = [b, -a] if sign > 0 else [-b, a]
            return jnp.concatenate([jnp.concatenate([a, b], axis=1), jnp.concatenate(low, axis=1)], axis=0)

        def right(a, b):
            first, second = ([a, b], [b, -a]) if sign > 0 else ([a, -b], [b, a])
            return jnp.concatenate([jnp.concatenate(first, axis=1), jnp.concatenate(second, axis=1)], axis=0)

        (re_hi, re_lo), (im_hi, im_lo) = split(re), split(im)
        hi, lo = left(re_hi, im_hi), left(re_lo, im_lo)
        mid = dot(t_hi, hi) + (dot(t_hi, lo) + dot(t_lo, hi))
        (re_hi, re_lo), (im_hi, im_lo) = split(mid[:, :n]), split(mid[:, n:])
        hi, lo = right(re_hi, im_hi), right(re_lo, im_lo)
        out = dot(hi, r_hi) + (dot(lo, r_hi) + dot(hi, r_lo))
        return out[:n], out[n:]

    count = grid(cnt_ref)
    cover = jnp.minimum(count, 1.0)
    scale = 1.0 / jnp.maximum(count, 1.0)
    obs_re = grid(sum_ref.at[0]) * scale
    obs_im = grid(sum_ref.at[1]) * scale
    re, im = obs_re, obs_im
    for step in range(ITERS):
        u_re = cover * obs_re + (1.0 - cover) * re
        u_im = cover * obs_im + (1.0 - cover) * im
        f_re, f_im = transform(1, u_re, u_im)
        power = f_re * f_re + f_im * f_im
        lam = 0.5 * (jnp.sum(power) / cells) + 1e-06
        keep = power / (power + lam)
        re, im = transform(-1, f_re * keep, f_im * keep)
        re, im = re * (1.0 / cells), im * (1.0 / cells)
    for part, value in enumerate((re, im)):
        for side in range(2):
            out_ref[pl.ds(2 * side + part, n, stride=4), :] = value[:, side * TILE:(side + 1) * TILE]


def mwni(sums, counts, tables):
    vmem = pl.BlockSpec(memory_space=pltpu.VMEM)
    return pl.pallas_call(
        mwni_kernel,
        out_shape=jax.ShapeDtypeStruct((1024, TILE), F32),
        in_specs=[vmem] * 3,
        out_specs=vmem,
        compiler_params=pltpu.CompilerParams(vmem_limit_bytes=56 * 1024 * 1024),
        name="mwni",
    )(sums, counts, tables)


def local(zn, table, tables, traces, bin_ids, valid, tile_owner):
    tiles = tile_owner.shape[0]
    sums, counts = observe(zn, traces, table, bin_ids.reshape(tiles, TILE), valid.reshape(tiles, TILE),
                           tile_owner.reshape(1, tiles))
    state = mwni(sums, counts.reshape(-1, TILE), tables)
    return state.reshape(-1, 2, TILE).transpose(1, 0, 2).reshape(1, 2, -1)


def solution(mesh):
    zn = mesh.shape["bins"] // YN
    table = dft_table(zn, 250)
    tables = grid_tables()
    in_specs = (P("freq", "bins"), P("bins"), P("bins"), P("bins", None))
    out_specs = P(("bins", "freq"), None, None)

    def run(traces, bin_ids, valid, tile_owner):
        return jax.shard_map(
            functools.partial(local, zn, jnp.asarray(table), jnp.asarray(tables)),
            mesh=mesh, in_specs=in_specs, out_specs=out_specs, check_vma=False,
        )(traces, bin_ids, valid, tile_owner)

    return run
```
